512 devices in a mesh: seq: 128 (over y, x_hi, z), chan: 4 (over x_lo, core).
Axes of the slice: x: 4 (x_hi: 2, x_lo: 2; x = x_hi * 2 + x_lo), y: 4, z: 16, core: 2. Of those that a mesh axis runs over, the one named last changes fastest.
Arguments:
- inputs: bfloat16 [128, 32768], P('chan', 'seq'), may hold values from -6 to 6
- gate_values: bfloat16 [128, 32768], P('chan', 'seq'), may hold values from -6 to 6
- filters: float32 [8, 32768], P('chan', 'seq'), may hold values from -5 to 5
- skip_weight: float32 [128], P('chan'), may hold values from -4 to 4
- grad_out: bfloat16 [128, 32768], P('chan', 'seq'), may hold values from -6 to 6
Outputs:
- grad_input: bfloat16 [128, 32768], P('chan', 'seq')
- grad_gate: bfloat16 [128, 32768], P('chan', 'seq')
- grad_filter: float32 [8, 32768], P('chan', 'seq')
The draws below stay inside these ranges and needn't reach their ends.
All inputs are finite; a program needn't handle non-finite values.
Results may differ from the reference program's by a relative error of at most 0.0014.
Values sent between devices are 32-bit elements; how exact they have to be, the bound alone decides.
No kernel may reach another device: no remote copies, remote signals or barrier semaphores. Data moves between devices by JAX's collectives and lax.ppermute only.
A program may use at most 64 MiB of HBM per device.

```python
import math
import jax
import jax.numpy as jnp

CH = 128
FILTER_GROUPS = 8
WINDOW_TOKENS = 32768


def draw_filters(key, part):
    key = jax.random.fold_in(key, 17)
    falloff_random_key, spike_random_key, jitter_random_key = jax.random.split(key, 3)
    steps_axis = jnp.arange(WINDOW_TOKENS, dtype=jnp.float32)[None, :]
    lengths = jnp.exp(jax.random.uniform(falloff_random_key, (FILTER_GROUPS, 1), minval=math.log(30.0), maxval=math.log(4.0 * WINDOW_TOKENS)))
    spike_location = jax.random.randint(spike_random_key, (FILTER_GROUPS, 3, 1), 0, WINDOW_TOKENS)
    token_positions = jnp.arange(WINDOW_TOKENS, dtype=jnp.int32)[None, None, :]
    dropped_entries = jnp.prod(jnp.where(token_positions >= spike_location, 0.6, 1.0), axis=1)
    roughness = jax.random.truncated_normal(jitter_random_key, -4.0, 4.0, (FILTER_GROUPS, WINDOW_TOKENS))
    amplitude = jnp.sqrt((1.0 - jnp.exp(-2.0 / lengths)) / (1.0 - jnp.exp(-2.0 * WINDOW_TOKENS / lengths)))
    return (amplitude * jnp.exp(-steps_axis / lengths) * dropped_entries * roughness).astype(jnp.float32)


def shard_levels(stream_key, dims, pieces, least, top_value):
    loudness, own = 1.0, jax.random.fold_in(stream_key, 6)
    for dim, blocks in pieces:
        steps = jnp.exp(jax.random.uniform(jax.random.fold_in(own, dim), (blocks,), jnp.float32, least / len(pieces), top_value / len(pieces)))
        loudness = loudness * jnp.repeat(steps, dims[dim] // blocks).reshape([-1 if axis == dim else 1 for axis in range(len(dims))])
    return loudness


def gaussian(own_key, extent, deviation, most, cuts=(), kind=jnp.bfloat16):
    array = jax.random.normal(own_key, extent, jnp.float32) * deviation
    if len(cuts) > 0:
        array = shard_levels(own_key, extent, cuts, -0.22, 0.18) * array
    return jnp.clip(array, min=-most, max=most).astype(kind)


def setup_inputs(seed: int = 0) -> dict:
    key_list = jax.random.split(jax.random.key(seed), 6)
    inputs = gaussian(key_list[0], (CH, WINDOW_TOKENS), 1.0, 6.0, ((0, 4), (1, 128)))
    gate_values = gaussian(key_list[1], (CH, WINDOW_TOKENS), 1.0, 6.0, ((0, 4), (1, 128)))
    filters = draw_filters(jax.random.fold_in(key_list[5], 71), 0)
    skip_weight = gaussian(key_list[3], (CH,), 1.0, 4.0, ((0, 4),), jnp.float32)
    grad_out = gaussian(key_list[4], (CH, WINDOW_TOKENS), 1.0, 6.0, ((0, 4), (1, 128)))
    return {"inputs": inputs, "gate_values": gate_values, "filters": filters, "skip_weight": skip_weight, "grad_out": grad_out}


def reference(inputs, gate_values, filters, skip_weight, grad_out):
    length = inputs.shape[1]
    transform_len = 2 * length
    signal = inputs.astype(jnp.float32)
    gate_float = gate_values.astype(jnp.float32)
    upstream = grad_out.astype(jnp.float32)
    filter_spectrum = jnp.fft.rfft(filters, n=transform_len, axis=1)
    per_channel = jnp.tile(filter_spectrum, (CH // FILTER_GROUPS, 1))
    input_spectrum = jnp.fft.rfft(signal, n=transform_len, axis=1)
    convolved = jnp.fft.irfft(input_spectrum * per_channel, n=transform_len, axis=1)[:, :length]
    convolved = convolved + skip_weight[:, None] * signal
    grad_mixed = upstream * gate_float
    grad_gate = (upstream * convolved).astype(jnp.bfloat16)
    pulled_spectrum = jnp.fft.rfft(grad_mixed, n=transform_len, axis=1)
    pulled = jnp.fft.irfft(pulled_spectrum * jnp.conj(per_channel), n=transform_len, axis=1)[:, :length]
    grad_input = (pulled + skip_weight[:, None] * grad_mixed).astype(jnp.bfloat16)
    cross_spectrum = (pulled_spectrum * jnp.conj(input_spectrum)).reshape(CH // FILTER_GROUPS, FILTER_GROUPS, -1).sum(axis=0)
    cross = jnp.fft.irfft(cross_spectrum, n=transform_len, axis=1)[:, :length]
    grad_filter = (cross / math.sqrt(length)).astype(jnp.float32)
    return (grad_input, grad_gate, grad_filter)
```

```python
import math

import jax
import jax.numpy as jnp
from jax import lax
from jax.experimental import pallas as pl
from jax.experimental.pallas import tpu as pltpu
from jax.sharding import PartitionSpec as P

BLOCK = 256
BLOCKS = 128
QUARTERS = 4
FINE = 16
PARTS = BLOCK // (QUARTERS * FINE)
STEPS = BLOCKS // FINE
F32 = jnp.float32
BF16 = jnp.bfloat16


def split(value):
    high = value.astype(BF16)
    return high, (value - high.astype(F32)).astype(BF16)


def rows_down(value):
    row = lax.broadcasted_iota(jnp.int32, value.shape, 0)
    return jnp.where(row == 0, 0.0, pltpu.roll(value, 1, 0))


def rows_up(value):
    row = lax.broadcasted_iota(jnp.int32, value.shape, 0)
    return jnp.where(row == BLOCKS - 1, 0.0, pltpu.roll(value, BLOCKS - 1, 0))


def nt_dot(left, right):
    return lax.dot_general(
        left, right, (((1,), (1,)), ((), ())), preferred_element_type=F32
    )


def window_rows(wide, start, store):
    turned = pltpu.roll(wide, (2 * BLOCK - start) % (2 * BLOCK), 1)
    half = pltpu.roll(turned, 2 * BLOCK - BLOCK // PARTS, 1)
    store(0, turned[:, :BLOCK])
    store(1, half[:, :BLOCK])
    store(2, turned[:, 128 : 128 + BLOCK])
    store(3, half[:, 128 : 128 + BLOCK])


def middle_kernel(r_ref, a_ref, out_ref, taps, windows, acc):
    r = r_ref[0]
    x = jnp.concatenate([a_ref[0], a_ref[1]], axis=1)
    g = jnp.concatenate([a_ref[2], a_ref[3]], axis=1)
    h = jnp.concatenate([a_ref[4], a_ref[5]], axis=1)
    h_down = rows_down(h)

    def keep(slot):
        def store(i, rows):
            high, low = split(rows)
            windows[slot, i] = high
            windows[slot + 1, i] = low

        return store

    window_rows(jnp.concatenate([g, rows_up(g)], axis=1), FINE * r, keep(0))
    window_rows(jnp.concatenate([h_down, h], axis=1), FINE * r + FINE, keep(2))

    def taps_of(slot, wide, shift_of, low_slot=None):
        for n in range(FINE):
            turned = pltpu.roll(wide, shift_of(n) % 384, 1) if shift_of(n) % 384 else wide
            value = turned[:, 128:]
            high, low = split(value)
            taps[slot, :, n] = high.reshape(STEPS, FINE, BLOCK)
            if low_slot is not None:
                taps[low_slot, :, n] = low.reshape(STEPS, FINE, BLOCK)

    x_down = rows_down(x)
    taps_of(0, jnp.concatenate([h_down[:, 128:], h], axis=1), lambda n: n, 1)
    taps_of(2, jnp.concatenate([x_down[:, 128:], x], axis=1), lambda n: n)
    lane = lax.broadcasted_iota(jnp.int32, (BLOCK, BLOCK), 1)
    row = lax.broadcasted_iota(jnp.int32, (BLOCK, BLOCK), 0)
    mirror = (lane + row == BLOCK - 1).astype(BF16)
    flipped = jnp.dot(x.astype(BF16), mirror, preferred_element_type=F32)
    flipped_down = rows_down(flipped)
    wide = jnp.concatenate([flipped, flipped_down[:, :128]], axis=1)
    taps_of(3, pltpu.roll(wide, 128, 1), lambda n: n - (FINE - 1))

    for step in range(STEPS):
        shift = FINE * step
        size = BLOCKS - shift

        def rhs(slot):
            return taps[slot, step].reshape(BLOCK, BLOCK)

        def lhs(slot, start):
            return windows[slot, :, start : start + size].reshape(PARTS * size, BLOCK)

        g_high, g_low = lhs(0, shift), lhs(1, shift)
        h_high, h_low = lhs(2, 0), lhs(3, 0)
        cross = nt_dot(g_high, rhs(2)) + nt_dot(g_low, rhs(2))
        pulled = nt_dot(g_high, rhs(0)) + nt_dot(g_low, rhs(0)) + nt_dot(g_high, rhs(1))
        conv = nt_dot(h_high, rhs(3)) + nt_dot(h_low, rhs(3))
        for slot, start, value in ((0, shift, conv), (1, 0, pulled), (2, 0, cross)):
            value = value.reshape(PARTS, size, BLOCK)
            if step == 0:
                acc[slot] = value
            else:
                acc[slot, :, start : start + size] = acc[slot, :, start : start + size] + value

    column = lax.broadcasted_iota(jnp.int32, (BLOCKS, BLOCK), 1) % FINE
    line = lax.broadcasted_iota(jnp.int32, (BLOCKS, BLOCK), 0)
    source = lax.broadcasted_iota(jnp.int32, (BLOCK, 128), 0)
    target = lax.broadcasted_iota(jnp.int32, (BLOCK, 128), 1)
    totals = [jnp.zeros((BLOCKS, 128), F32), jnp.zeros((BLOCKS, 128), F32)]
    for slot, page, offset in ((0, 0, 0), (1, 0, 64), (2, 1, 0)):
        total = totals[page]
        for i in range(PARTS):
            value = acc[slot, i]
            for bit in (1, 2, 4, 8):
                if slot == 0:
                    moved = jnp.where(line < bit, 0.0, pltpu.roll(value, bit, 0))
                else:
                    moved = jnp.where(line >= BLOCKS - bit, 0.0, pltpu.roll(value, BLOCKS - bit, 0))
                value = jnp.where((column & bit) != 0, moved, value)
            pick = (source // FINE + FINE * i + offset == target).astype(BF16)
            high, low = split(value)
            total = total + jnp.dot(high, pick, preferred_element_type=F32)
            total = total + jnp.dot(low, pick, preferred_element_type=F32)
        totals[page] = total
    out_ref[0] = totals[0]
    out_ref[1] = totals[1]


def middle(arrived, r):
    return pl.pallas_call(
        middle_kernel,
        out_shape=jax.ShapeDtypeStruct((2, BLOCKS, 128), F32),
        in_specs=[
            pl.BlockSpec(memory_space=pltpu.SMEM),
            pl.BlockSpec(memory_space=pltpu.VMEM),
        ],
        out_specs=pl.BlockSpec(memory_space=pltpu.VMEM),
        scratch_shapes=[
            pltpu.VMEM((4, STEPS, FINE, FINE, BLOCK), BF16),
            pltpu.VMEM((4, PARTS, BLOCKS, BLOCK), BF16),
            pltpu.VMEM((3, PARTS, BLOCKS, BLOCK), F32),
        ],
        compiler_params=pltpu.CompilerParams(vmem_limit_bytes=48 * 1024 * 1024),
    )(r, arrived)


def source_kernel(x_ref, gate_ref, up_ref, filter_ref, out_ref):
    x = x_ref[...].astype(F32)
    mixed = up_ref[...].astype(F32) * gate_ref[...].astype(F32)
    filters = jnp.concatenate([filter_ref[...]] * 4, axis=0)
    for page, value in ((0, x), (2, mixed), (4, filters)):
        for half in range(2):
            part = value[:, 128 * half : 128 * half + 128]
            for quarter in range(QUARTERS):
                out_ref[page + half, 32 * quarter : 32 * quarter + 32] = part


def source(x, gate, up, filters):
    return pl.pallas_call(
        source_kernel,
        out_shape=jax.ShapeDtypeStruct((6, BLOCKS, 128), F32),
    )(x, gate, up, filters)


def exact_dot(value, pick):
    high = value.astype(BF16)
    rest = value - high.astype(F32)
    mid = rest.astype(BF16)
    low = (rest - mid.astype(F32)).astype(BF16)
    total = jnp.dot(high, pick, preferred_element_type=F32)
    total = total + jnp.dot(mid, pick, preferred_element_type=F32)
    return total + jnp.dot(low, pick, preferred_element_type=F32)


def final_kernel(b_ref, x_ref, gate_ref, up_ref, skip_ref, gi_ref, gg_ref, gf_ref):
    source = lax.broadcasted_iota(jnp.int32, (128, 2 * BLOCK), 0)
    target = lax.broadcasted_iota(jnp.int32, (128, 2 * BLOCK), 1)
    both = jnp.zeros((32, 2 * BLOCK), F32)
    taps = jnp.zeros((8, BLOCK), F32)
    for quarter in range(QUARTERS):
        place = (source // FINE) * (BLOCK // PARTS) + FINE * quarter + source % FINE
        pick = (place == target).astype(BF16)
        both = both + exact_dot(b_ref[0, 32 * quarter : 32 * quarter + 32], pick)
        cross = b_ref[1, 32 * quarter : 32 * quarter + 32].reshape(4, 8, 128).sum(axis=0)
        taps = taps + exact_dot(cross, pick[:, :BLOCK])
    x = x_ref[...].astype(F32)
    up = up_ref[...].astype(F32)
    mixed = up * gate_ref[...].astype(F32)
    skip = skip_ref[...]
    gg_ref[...] = (up * (both[:, :BLOCK] + skip * x)).astype(BF16)
    gi_ref[...] = (both[:, BLOCK:] + skip * mixed).astype(BF16)
    gf_ref[...] = taps * (1.0 / math.sqrt(BLOCKS * BLOCK))


def final(returned, x, gate, up, skip):
    piece = jax.ShapeDtypeStruct((32, BLOCK), BF16)
    return pl.pallas_call(
        final_kernel,
        out_shape=(piece, piece, jax.ShapeDtypeStruct((8, BLOCK), F32)),
    )(returned, x, gate, up, skip)


def body(inputs, gate_values, filters, skip_weight, grad_out):
    quarter = (lax.axis_index("seq") // 32).astype(jnp.int32).reshape(1)
    every_filter = lax.all_gather(filters, "chan", axis=0, tiled=True)
    leaving = source(inputs, gate_values, grad_out, every_filter)
    arrived = lax.all_to_all(leaving, "seq", split_axis=1, concat_axis=1, tiled=True)
    results = middle(arrived, quarter)
    returned = lax.all_to_all(results, "seq", split_axis=1, concat_axis=1, tiled=True)
    grad_input, grad_gate, taps = final(
        returned, inputs, gate_values, grad_out, skip_weight[:, None]
    )
    grad_filter = lax.psum_scatter(taps, "chan", scatter_dimension=0, tiled=True)
    return (grad_input, grad_gate, grad_filter)


def solution(mesh):
    placed = (P("chan", "seq"), P("chan", "seq"), P("chan", "seq"), P("chan"), P("chan", "seq"))
    return jax.shard_map(
        body,
        mesh=mesh,
        in_specs=placed,
        out_specs=(P("chan", "seq"), P("chan", "seq"), P("chan", "seq")),
        check_vma=False,
    )
```

```python
import math

import jax
import jax.numpy as jnp
from jax import lax
from jax.experimental import pallas as pl
from jax.experimental.pallas import tpu as pltpu
from jax.sharding import PartitionSpec as P

BLOCK = 256
BLOCKS = 128
QUARTERS = 4
FINE = 16
PARTS = BLOCK // (QUARTERS * FINE)
STEPS = BLOCKS // FINE
F32 = jnp.float32
BF16 = jnp.bfloat16


def split(value):
    high = value.astype(BF16)
    return high, (value - high.astype(F32)).astype(BF16)


def rows_down(value):
    row = lax.broadcasted_iota(jnp.int32, value.shape, 0)
    return jnp.where(row == 0, 0.0, pltpu.roll(value, 1, 0))


def rows_up(value):
    row = lax.broadcasted_iota(jnp.int32, value.shape, 0)
    return jnp.where(row == BLOCKS - 1, 0.0, pltpu.roll(value, BLOCKS - 1, 0))


def nt_dot(left, right):
    return lax.dot_general(
        left, right, (((1,), (1,)), ((), ())), preferred_element_type=F32
    )


def window_rows(wide, start, store):
    turned = pltpu.roll(wide, (2 * BLOCK - start) % (2 * BLOCK), 1)
    half = pltpu.roll(turned, 2 * BLOCK - BLOCK // PARTS, 1)
    store(0, turned[:, :BLOCK])
    store(1, half[:, :BLOCK])
    store(2, turned[:, 128 : 128 + BLOCK])
    store(3, half[:, 128 : 128 + BLOCK])


def middle_kernel(r_ref, a_ref, out_ref, taps, windows, acc):
    r = r_ref[0]

    def signal(first):
        halves = [a_ref[:, first + half].reshape(BLOCKS, 128) for half in range(2)]
        return jnp.concatenate(halves, axis=1)

    x, g, h = signal(0), signal(2), signal(4)
    h_down = rows_down(h)

    def keep(slot):
        def store(i, rows):
            high, low = split(rows)
            windows[slot, i] = high
            windows[slot + 1, i] = low

        return store

    window_rows(jnp.concatenate([g, rows_up(g)], axis=1), FINE * r, keep(0))
    window_rows(jnp.concatenate([h_down, h], axis=1), FINE * r + FINE, keep(2))

    def taps_of(slot, wide, shift_of, low_slot=None):
        for n in range(FINE):
            turned = pltpu.roll(wide, shift_of(n) % 384, 1) if shift_of(n) % 384 else wide
            value = turned[:, 128:]
            high, low = split(value)
            taps[slot, :, n] = high.reshape(STEPS, FINE, BLOCK)
            if low_slot is not None:
                taps[low_slot, :, n] = low.reshape(STEPS, FINE, BLOCK)

    x_down = rows_down(x)
    taps_of(0, jnp.concatenate([h_down[:, 128:], h], axis=1), lambda n: n, 1)
    taps_of(2, jnp.concatenate([x_down[:, 128:], x], axis=1), lambda n: n)
    lane = lax.broadcasted_iota(jnp.int32, (BLOCK, BLOCK), 1)
    row = lax.broadcasted_iota(jnp.int32, (BLOCK, BLOCK), 0)
    mirror = (lane + row == BLOCK - 1).astype(BF16)
    flipped = jnp.dot(x.astype(BF16), mirror, preferred_element_type=F32)
    flipped_down = rows_down(flipped)
    wide = jnp.concatenate([flipped, flipped_down[:, :128]], axis=1)
    taps_of(3, pltpu.roll(wide, 128, 1), lambda n: n - (FINE - 1))

    for step in range(STEPS):
        shift = FINE * step
        size = BLOCKS - shift

        def rhs(slot):
            return taps[slot, step].reshape(BLOCK, BLOCK)

        def lhs(slot, start):
            return windows[slot, :, start : start + size].reshape(PARTS * size, BLOCK)

        g_high, g_low = lhs(0, shift), lhs(1, shift)
        h_high, h_low = lhs(2, 0), lhs(3, 0)
        cross = nt_dot(g_high, rhs(2)) + nt_dot(g_low, rhs(2))
        pulled = nt_dot(g_high, rhs(0)) + nt_dot(g_low, rhs(0)) + nt_dot(g_high, rhs(1))
        conv = nt_dot(h_high, rhs(3)) + nt_dot(h_low, rhs(3))
        for slot, start, value in ((0, shift, conv), (1, 0, pulled), (2, 0, cross)):
            value = value.reshape(PARTS, size, BLOCK)
            if step == 0:
                acc[slot] = value
            else:
                acc[slot, :, start : start + size] = acc[slot, :, start : start + size] + value

    column = lax.broadcasted_iota(jnp.int32, (BLOCKS, BLOCK), 1) % FINE
    line = lax.broadcasted_iota(jnp.int32, (BLOCKS, BLOCK), 0)
    source = lax.broadcasted_iota(jnp.int32, (BLOCK, 128), 0)
    target = lax.broadcasted_iota(jnp.int32, (BLOCK, 128), 1)
    totals = [jnp.zeros((BLOCKS, 128), F32), jnp.zeros((BLOCKS, 128), F32)]
    for slot, page, offset in ((0, 0, 0), (1, 0, 64), (2, 1, 0)):
        total = totals[page]
        for i in range(PARTS):
            value = acc[slot, i]
            for bit in (1, 2, 4, 8):
                if slot == 0:
                    moved = jnp.where(line < bit, 0.0, pltpu.roll(value, bit, 0))
                else:
                    moved = jnp.where(line >= BLOCKS - bit, 0.0, pltpu.roll(value, BLOCKS - bit, 0))
                value = jnp.where((column & bit) != 0, moved, value)
            pick = (source // FINE + FINE * i + offset == target).astype(BF16)
            high, low = split(value)
            total = total + jnp.dot(high, pick, preferred_element_type=F32)
            total = total + jnp.dot(low, pick, preferred_element_type=F32)
        totals[page] = total
    out_ref[:, 0] = totals[0]
    out_ref[:, 1] = totals[1]


def middle(arrived, r):
    return pl.pallas_call(
        middle_kernel,
        out_shape=jax.ShapeDtypeStruct((BLOCKS, 2, 128), F32),
        in_specs=[
            pl.BlockSpec(memory_space=pltpu.SMEM),
            pl.BlockSpec(memory_space=pltpu.VMEM),
        ],
        out_specs=pl.BlockSpec(memory_space=pltpu.VMEM),
        scratch_shapes=[
            pltpu.VMEM((4, STEPS, FINE, FINE, BLOCK), BF16),
            pltpu.VMEM((4, PARTS, BLOCKS, BLOCK), BF16),
            pltpu.VMEM((3, PARTS, BLOCKS, BLOCK), F32),
        ],
        compiler_params=pltpu.CompilerParams(vmem_limit_bytes=48 * 1024 * 1024),
    )(r, arrived)


RING = 16
PLANES = 8


def source_kernel(x_ref, gate_ref, up_ref, filter_ref, out_ref):
    x = x_ref[...].astype(F32)
    mixed = up_ref[...].astype(F32) * gate_ref[...].astype(F32)
    filters = jnp.concatenate([filter_ref[i] for i in range(4)] * 2, axis=0)
    line = 0
    for value in (x[:RING], x[RING:], mixed[:RING], mixed[RING:], filters):
        for half in range(2):
            out_ref[:, line] = value[:, 128 * half : 128 * half + 128]
            line += 1
    out_ref[:, line:] = jnp.zeros((RING, 16 - line, 128), F32)


def source(x, gate, up, filters):
    return pl.pallas_call(
        source_kernel,
        out_shape=jax.ShapeDtypeStruct((RING, 16, 128), F32),
    )(x, gate, up, filters)


def spread_kernel(in_ref, out_ref):
    lines = [in_ref[:, line] for line in range(10)]
    for plane in range(PLANES):
        member = plane % 2
        chosen = (2 * member, 2 * member + 1, 4 + 2 * member, 5 + 2 * member, 8, 9)
        for place, line in enumerate(chosen):
            out_ref[plane, place] = lines[line]


def spread(ring):
    return pl.pallas_call(
        spread_kernel,
        out_shape=jax.ShapeDtypeStruct((PLANES, 6, RING, 128), F32),
    )(ring)


def exact_dot(value, pick):
    high = value.astype(BF16)
    rest = value - high.astype(F32)
    mid = rest.astype(BF16)
    low = (rest - mid.astype(F32)).astype(BF16)
    total = jnp.dot(high, pick, preferred_element_type=F32)
    total = total + jnp.dot(mid, pick, preferred_element_type=F32)
    return total + jnp.dot(low, pick, preferred_element_type=F32)


def quarter_pick(quarter, width):
    source = lax.broadcasted_iota(jnp.int32, (128, width), 0)
    target = lax.broadcasted_iota(jnp.int32, (128, width), 1)
    place = (source // FINE) * (BLOCK // PARTS) + FINE * quarter + source % FINE
    return (place == target).astype(BF16)


def taps_kernel(b_ref, gf_ref):
    taps = jnp.zeros((8, BLOCK), F32)
    for quarter in range(QUARTERS):
        cross = b_ref[32 * quarter : 32 * quarter + 32, 1].reshape(4, 8, 128).sum(axis=0)
        taps = taps + exact_dot(cross, quarter_pick(quarter, BLOCK))
    gf_ref[...] = taps * (1.0 / math.sqrt(BLOCKS * BLOCK))


def final_taps(returned):
    return pl.pallas_call(
        taps_kernel, out_shape=jax.ShapeDtypeStruct((8, BLOCK), F32)
    )(returned)


def final_kernel(b_ref, x_ref, gate_ref, up_ref, skip_ref, gi_ref, gg_ref):
    both = jnp.zeros((32, 2 * BLOCK), F32)
    for quarter in range(QUARTERS):
        rows = b_ref[32 * quarter : 32 * quarter + 32, 0]
        both = both + exact_dot(rows, quarter_pick(quarter, 2 * BLOCK))
    x = x_ref[...].astype(F32)
    up = up_ref[...].astype(F32)
    mixed = up * gate_ref[...].astype(F32)
    skip = skip_ref[...]
    gg_ref[...] = (up * (both[:, :BLOCK] + skip * x)).astype(BF16)
    gi_ref[...] = (both[:, BLOCK:] + skip * mixed).astype(BF16)


def final(returned, x, gate, up, skip):
    piece = jax.ShapeDtypeStruct((32, BLOCK), BF16)
    return pl.pallas_call(final_kernel, out_shape=(piece, piece))(returned, x, gate, up, skip)


def body(inputs, gate_values, filters, skip_weight, grad_out):
    quarter = (lax.axis_index("seq") >> 5).astype(jnp.int32).reshape(1)
    rings = [[RING * plane + z for z in range(RING)] for plane in range(PLANES)]
    planes = [[RING * plane + z for plane in range(PLANES)] for z in range(RING)]
    every_filter = lax.all_gather(filters, "chan", axis=0)
    leaving = source(inputs, gate_values, grad_out, every_filter)
    ring = lax.all_to_all(
        leaving, "seq", split_axis=0, concat_axis=0, tiled=True, axis_index_groups=rings
    )
    arrived = lax.all_to_all(
        spread(ring), "seq", split_axis=0, concat_axis=0, tiled=True, axis_index_groups=planes
    )
    results = middle(arrived, quarter)
    returned = lax.all_to_all(results, "seq", split_axis=0, concat_axis=0, tiled=True)
    taps = final_taps(returned)
    grad_filter = lax.psum_scatter(taps, "chan", scatter_dimension=0, tiled=True)
    grad_input, grad_gate = final(
        returned, inputs, gate_values, grad_out, skip_weight[:, None]
    )
    return (grad_input, grad_gate, grad_filter)


def solution(mesh):
    placed = (P("chan", "seq"), P("chan", "seq"), P("chan", "seq"), P("chan"), P("chan", "seq"))
    return jax.shard_map(
        body,
        mesh=mesh,
        in_specs=placed,
        out_specs=(P("chan", "seq"), P("chan", "seq"), P("chan", "seq")),
        check_vma=False,
    )
```

```python
import math

import jax
import jax.numpy as jnp
from jax import lax
from jax.experimental import pallas as pl
from jax.experimental.pallas import tpu as pltpu
from jax.sharding import PartitionSpec as P

BLOCK = 256
BLOCKS = 128
QUARTERS = 4
FINE = 16
PARTS = BLOCK // (QUARTERS * FINE)
STEPS = BLOCKS // FINE
F32 = jnp.float32
BF16 = jnp.bfloat16


def split(value):
    high = value.astype(BF16)
    return high, (value - high.astype(F32)).astype(BF16)


def rows_down(value):
    row = lax.broadcasted_iota(jnp.int32, value.shape, 0)
    return jnp.where(row == 0, 0.0, pltpu.roll(value, 1, 0))


def rows_up(value):
    row = lax.broadcasted_iota(jnp.int32, value.shape, 0)
    return jnp.where(row == BLOCKS - 1, 0.0, pltpu.roll(value, BLOCKS - 1, 0))


def nt_dot(left, right):
    return lax.dot_general(
        left, right, (((1,), (1,)), ((), ())), preferred_element_type=F32
    )


def window_rows(wide, start, store):
    turned = pltpu.roll(wide, (2 * BLOCK - start) % (2 * BLOCK), 1)
    half = pltpu.roll(turned, 2 * BLOCK - BLOCK // PARTS, 1)
    store(0, turned[:, :BLOCK])
    store(1, half[:, :BLOCK])
    store(2, turned[:, 128 : 128 + BLOCK])
    store(3, half[:, 128 : 128 + BLOCK])


def middle_kernel(r_ref, a_ref, out_ref, taps, windows, acc):
    r = r_ref[0]

    def signal(first):
        halves = [a_ref[pl.ds(first + half, BLOCKS, stride=6), :] for half in range(2)]
        return jnp.concatenate(halves, axis=1)

    x, g, h = signal(0), signal(2), signal(4)
    h_down = rows_down(h)

    def keep(slot):
        def store(i, rows):
            high, low = split(rows)
            windows[slot, i] = high
            windows[slot + 1, i] = low

        return store

    window_rows(jnp.concatenate([g, rows_up(g)], axis=1), FINE * r, keep(0))
    window_rows(jnp.concatenate([h_down, h], axis=1), FINE * r + FINE, keep(2))

    def taps_of(slot, wide, shift_of, low_slot=None):
        for n in range(FINE):
            turned = pltpu.roll(wide, shift_of(n) % 384, 1) if shift_of(n) % 384 else wide
            value = turned[:, 128:]
            high, low = split(value)
            taps[slot, :, n] = high.reshape(STEPS, FINE, BLOCK)
            if low_slot is not None:
                taps[low_slot, :, n] = low.reshape(STEPS, FINE, BLOCK)

    x_down = rows_down(x)
    taps_of(0, jnp.concatenate([h_down[:, 128:], h], axis=1), lambda n: n, 1)
    taps_of(2, jnp.concatenate([x_down[:, 128:], x], axis=1), lambda n: n)
    lane = lax.broadcasted_iota(jnp.int32, (BLOCK, BLOCK), 1)
    row = lax.broadcasted_iota(jnp.int32, (BLOCK, BLOCK), 0)
    mirror = (lane + row == BLOCK - 1).astype(BF16)
    flipped = jnp.dot(x.astype(BF16), mirror, preferred_element_type=F32)
    flipped_down = rows_down(flipped)
    wide = jnp.concatenate([flipped, flipped_down[:, :128]], axis=1)
    taps_of(3, pltpu.roll(wide, 128, 1), lambda n: n - (FINE - 1))

    for step in range(STEPS):
        shift = FINE * step
        size = BLOCKS - shift

        def rhs(slot):
            return taps[slot, step].reshape(BLOCK, BLOCK)

        def lhs(slot, start):
            return windows[slot, :, start : start + size].reshape(PARTS * size, BLOCK)

        g_high, g_low = lhs(0, shift), lhs(1, shift)
        h_high, h_low = lhs(2, 0), lhs(3, 0)
        cross = nt_dot(g_high, rhs(2)) + nt_dot(g_low, rhs(2))
        pulled = nt_dot(g_high, rhs(0)) + nt_dot(g_low, rhs(0)) + nt_dot(g_high, rhs(1))
        conv = nt_dot(h_high, rhs(3)) + nt_dot(h_low, rhs(3))
        for slot, start, value in ((0, shift, conv), (1, 0, pulled), (2, 0, cross)):
            value = value.reshape(PARTS, size, BLOCK)
            if step == 0:
                acc[slot] = value
            else:
                acc[slot, :, start : start + size] = acc[slot, :, start : start + size] + value

    column = lax.broadcasted_iota(jnp.int32, (BLOCKS, BLOCK), 1) % FINE
    line = lax.broadcasted_iota(jnp.int32, (BLOCKS, BLOCK), 0)
    source = lax.broadcasted_iota(jnp.int32, (BLOCK, 128), 0)
    target = lax.broadcasted_iota(jnp.int32, (BLOCK, 128), 1)
    totals = [jnp.zeros((BLOCKS, 128), F32), jnp.zeros((BLOCKS, 128), F32)]
    for slot, page, offset in ((0, 0, 0), (1, 0, 64), (2, 1, 0)):
        total = totals[page]
        for i in range(PARTS):
            value = acc[slot, i]
            for bit in (1, 2, 4, 8):
                if slot == 0:
                    moved = jnp.where(line < bit, 0.0, pltpu.roll(value, bit, 0))
                else:
                    moved = jnp.where(line >= BLOCKS - bit, 0.0, pltpu.roll(value, BLOCKS - bit, 0))
                value = jnp.where((column & bit) != 0, moved, value)
            pick = (source // FINE + FINE * i + offset == target).astype(BF16)
            high, low = split(value)
            total = total + jnp.dot(high, pick, preferred_element_type=F32)
            total = total + jnp.dot(low, pick, preferred_element_type=F32)
        totals[page] = total
    out_ref[pl.ds(0, BLOCKS, stride=2), :] = totals[0]
    out_ref[pl.ds(1, BLOCKS, stride=2), :] = totals[1]


def middle(arrived, r):
    return pl.pallas_call(
        middle_kernel,
        out_shape=jax.ShapeDtypeStruct((2 * BLOCKS, 128), F32),
        in_specs=[
            pl.BlockSpec(memory_space=pltpu.SMEM),
            pl.BlockSpec(memory_space=pltpu.VMEM),
        ],
        out_specs=pl.BlockSpec(memory_space=pltpu.VMEM),
        scratch_shapes=[
            pltpu.VMEM((4, STEPS, FINE, FINE, BLOCK), BF16),
            pltpu.VMEM((4, PARTS, BLOCKS, BLOCK), BF16),
            pltpu.VMEM((3, PARTS, BLOCKS, BLOCK), F32),
        ],
        compiler_params=pltpu.CompilerParams(vmem_limit_bytes=48 * 1024 * 1024),
    )(r, arrived)


VMEM = pl.BlockSpec(memory_space=pltpu.VMEM)


def source_kernel(x_ref, gate_ref, up_ref, filter_ref, out_ref):
    x = x_ref[...].astype(F32)
    mixed = up_ref[...].astype(F32) * gate_ref[...].astype(F32)
    filters = jnp.concatenate([filter_ref[i] for i in range(4)] * 4, axis=0)
    line = 0
    for value in (x, mixed, filters):
        for half in range(2):
            part = value[:, 128 * half : 128 * half + 128]
            part = jnp.concatenate([part] * QUARTERS, axis=0)
            out_ref[pl.ds(line, BLOCKS, stride=6), :] = part
            line += 1


def source(x, gate, up, filters):
    return pl.pallas_call(
        source_kernel,
        out_shape=jax.ShapeDtypeStruct((6 * BLOCKS, 128), F32),
        in_specs=[VMEM] * 4,
        out_specs=VMEM,
    )(x, gate, up, filters)


def exact_dot(value, pick):
    high = value.astype(BF16)
    rest = value - high.astype(F32)
    mid = rest.astype(BF16)
    low = (rest - mid.astype(F32)).astype(BF16)
    total = jnp.dot(high, pick, preferred_element_type=F32)
    total = total + jnp.dot(mid, pick, preferred_element_type=F32)
    return total + jnp.dot(low, pick, preferred_element_type=F32)


def quarter_pick(quarter, width):
    source = lax.broadcasted_iota(jnp.int32, (128, width), 0)
    target = lax.broadcasted_iota(jnp.int32, (128, width), 1)
    place = (source // FINE) * (BLOCK // PARTS) + FINE * quarter + source % FINE
    return (place == target).astype(BF16)


def sums_kernel(b_ref, out_ref):
    for quarter in range(QUARTERS):
        rows = b_ref[pl.ds(64 * quarter + 1, 32, stride=2), :]
        total = rows.reshape(4, 8, 128).sum(axis=0)
        for owner in range(4):
            out_ref[owner, 2 * quarter : 2 * quarter + 2] = total[2 * owner : 2 * owner + 2]


def sums(returned):
    return pl.pallas_call(
        sums_kernel,
        out_shape=jax.ShapeDtypeStruct((4, 8, 128), F32),
        in_specs=[VMEM],
        out_specs=VMEM,
    )(returned)


def taps_kernel(b_ref, gf_ref):
    taps = jnp.zeros((2, BLOCK), F32)
    cross = (b_ref[0] + b_ref[1]) + (b_ref[2] + b_ref[3])
    for quarter in range(QUARTERS):
        taps = taps + exact_dot(cross[2 * quarter : 2 * quarter + 2], quarter_pick(quarter, BLOCK))
    gf_ref[...] = taps * (1.0 / math.sqrt(BLOCKS * BLOCK))


def final_taps(parts):
    return pl.pallas_call(
        taps_kernel,
        out_shape=jax.ShapeDtypeStruct((2, BLOCK), F32),
        in_specs=[VMEM],
        out_specs=VMEM,
    )(parts)


def final_kernel(b_ref, x_ref, gate_ref, up_ref, skip_ref, gi_ref, gg_ref):
    both = jnp.zeros((32, 2 * BLOCK), F32)
    for quarter in range(QUARTERS):
        rows = b_ref[pl.ds(64 * quarter, 32, stride=2), :]
        both = both + exact_dot(rows, quarter_pick(quarter, 2 * BLOCK))
    x = x_ref[...].astype(F32)
    up = up_ref[...].astype(F32)
    mixed = up * gate_ref[...].astype(F32)
    skip = skip_ref[...]
    gg_ref[...] = (up * (both[:, :BLOCK] + skip * x)).astype(BF16)
    gi_ref[...] = (both[:, BLOCK:] + skip * mixed).astype(BF16)


def final(returned, x, gate, up, skip):
    piece = jax.ShapeDtypeStruct((32, BLOCK), BF16)
    return pl.pallas_call(
        final_kernel,
        out_shape=(piece, piece),
        in_specs=[VMEM] * 5,
        out_specs=[VMEM] * 2,
    )(returned, x, gate, up, skip)


def exchange(rows):
    flat = rows.reshape(BLOCKS, 1, -1)
    flat = lax.all_to_all(flat, "seq", split_axis=0, concat_axis=0, tiled=True)
    return flat.reshape(rows.shape)


def body(inputs, gate_values, filters, skip_weight, grad_out):
    quarter = (lax.axis_index("seq") >> 5).astype(jnp.int32).reshape(1)
    every_filter = lax.all_gather(filters, "chan", axis=0)
    leaving = source(inputs, gate_values, grad_out, every_filter)
    results = middle(exchange(leaving), quarter)
    returned = exchange(results)
    shares = lax.all_to_all(sums(returned), "chan", split_axis=0, concat_axis=0, tiled=True)
    grad_input, grad_gate = final(
        returned, inputs, gate_values, grad_out, skip_weight[:, None]
    )
    return (grad_input, grad_gate, final_taps(shares))


def solution(mesh):
    placed = (P("chan", "seq"), P("chan", "seq"), P("chan", "seq"), P("chan"), P("chan", "seq"))
    return jax.shard_map(
        body,
        mesh=mesh,
        in_specs=placed,
        out_specs=(P("chan", "seq"), P("chan", "seq"), P("chan", "seq")),
        check_vma=False,
    )
```

```python
import math

import jax
import jax.numpy as jnp
from jax import lax
from jax.experimental import pallas as pl
from jax.experimental.pallas import tpu as pltpu
from jax.sharding import PartitionSpec as P

BLOCK = 256
BLOCKS = 128
QUARTERS = 4
FINE = 16
PARTS = BLOCK // (QUARTERS * FINE)
STEPS = BLOCKS // FINE
F32 = jnp.float32
BF16 = jnp.bfloat16


def split(value):
    high = value.astype(BF16)
    return high, (value - high.astype(F32)).astype(BF16)


def rows_down(value):
    row = lax.broadcasted_iota(jnp.int32, value.shape, 0)
    return jnp.where(row == 0, 0.0, pltpu.roll(value, 1, 0))


def rows_up(value):
    row = lax.broadcasted_iota(jnp.int32, value.shape, 0)
    return jnp.where(row == BLOCKS - 1, 0.0, pltpu.roll(value, BLOCKS - 1, 0))


def nt_dot(left, right):
    return lax.dot_general(
        left, right, (((1,), (1,)), ((), ())), preferred_element_type=F32
    )


def window_rows(wide, start, store):
    turned = pltpu.roll(wide, (2 * BLOCK - start) % (2 * BLOCK), 1)
    half = pltpu.roll(turned, 2 * BLOCK - BLOCK // PARTS, 1)
    store(0, turned[:, :BLOCK])
    store(1, half[:, :BLOCK])
    store(2, turned[:, 128 : 128 + BLOCK])
    store(3, half[:, 128 : 128 + BLOCK])


def middle_kernel(r_ref, a_ref, out_ref, taps, windows, acc):
    r = r_ref[0]

    def signal(first):
        halves = [a_ref[:, first + half].reshape(BLOCKS, 128) for half in range(2)]
        return jnp.concatenate(halves, axis=1)

    x, g, h = signal(0), signal(2), signal(4)
    h_down = rows_down(h)

    def keep(slot):
        def store(i, rows):
            high, low = split(rows)
            windows[slot, i] = high
            windows[slot + 1, i] = low

        return store

    window_rows(jnp.concatenate([g, rows_up(g)], axis=1), FINE * r, keep(0))
    window_rows(jnp.concatenate([h_down, h], axis=1), FINE * r + FINE, keep(2))

    def taps_of(slot, wide, shift_of, low_slot=None):
        for n in range(FINE):
            turned = pltpu.roll(wide, shift_of(n) % 384, 1) if shift_of(n) % 384 else wide
            value = turned[:, 128:]
            high, low = split(value)
            taps[slot, :, n] = high.reshape(STEPS, FINE, BLOCK)
            if low_slot is not None:
                taps[low_slot, :, n] = low.reshape(STEPS, FINE, BLOCK)

    x_down = rows_down(x)
    taps_of(0, jnp.concatenate([h_down[:, 128:], h], axis=1), lambda n: n, 1)
    taps_of(2, jnp.concatenate([x_down[:, 128:], x], axis=1), lambda n: n)
    lane = lax.broadcasted_iota(jnp.int32, (BLOCK, BLOCK), 1)
    row = lax.broadcasted_iota(jnp.int32, (BLOCK, BLOCK), 0)
    mirror = (lane + row == BLOCK - 1).astype(BF16)
    flipped = jnp.dot(x.astype(BF16), mirror, preferred_element_type=F32)
    flipped_down = rows_down(flipped)
    wide = jnp.concatenate([flipped, flipped_down[:, :128]], axis=1)
    taps_of(3, pltpu.roll(wide, 128, 1), lambda n: n - (FINE - 1))

    for step in range(STEPS):
        shift = FINE * step
        size = BLOCKS - shift

        def rhs(slot):
            return taps[slot, step].reshape(BLOCK, BLOCK)

        def lhs(slot, start):
            return windows[slot, :, start : start + size].reshape(PARTS * size, BLOCK)

        g_high, g_low = lhs(0, shift), lhs(1, shift)
        h_high, h_low = lhs(2, 0), lhs(3, 0)
        cross = nt_dot(g_high, rhs(2)) + nt_dot(g_low, rhs(2))
        pulled = nt_dot(g_high, rhs(0)) + nt_dot(g_low, rhs(0)) + nt_dot(g_high, rhs(1))
        conv = nt_dot(h_high, rhs(3)) + nt_dot(h_low, rhs(3))
        for slot, start, value in ((0, shift, conv), (1, 0, pulled), (2, 0, cross)):
            value = value.reshape(PARTS, size, BLOCK)
            if step == 0:
                acc[slot] = value
            else:
                acc[slot, :, start : start + size] = acc[slot, :, start : start + size] + value

    column = lax.broadcasted_iota(jnp.int32, (BLOCKS, BLOCK), 1) % FINE
    line = lax.broadcasted_iota(jnp.int32, (BLOCKS, BLOCK), 0)
    source = lax.broadcasted_iota(jnp.int32, (BLOCK, 128), 0)
    target = lax.broadcasted_iota(jnp.int32, (BLOCK, 128), 1)
    totals = [jnp.zeros((BLOCKS, 128), F32), jnp.zeros((BLOCKS, 128), F32)]
    for slot, page, offset in ((0, 0, 0), (1, 0, 64), (2, 1, 0)):
        total = totals[page]
        for i in range(PARTS):
            value = acc[slot, i]
            for bit in (1, 2, 4, 8):
                if slot == 0:
                    moved = jnp.where(line < bit, 0.0, pltpu.roll(value, bit, 0))
                else:
                    moved = jnp.where(line >= BLOCKS - bit, 0.0, pltpu.roll(value, BLOCKS - bit, 0))
                value = jnp.where((column & bit) != 0, moved, value)
            pick = (source // FINE + FINE * i + offset == target).astype(BF16)
            high, low = split(value)
            total = total + jnp.dot(high, pick, preferred_element_type=F32)
            total = total + jnp.dot(low, pick, preferred_element_type=F32)
        totals[page] = total
    out_ref[pl.ds(0, BLOCKS, stride=2), :] = totals[0]
    out_ref[pl.ds(1, BLOCKS, stride=2), :] = totals[1]


def middle(arrived, r):
    return pl.pallas_call(
        middle_kernel,
        out_shape=jax.ShapeDtypeStruct((2 * BLOCKS, 128), F32),
        in_specs=[
            pl.BlockSpec(memory_space=pltpu.SMEM),
            pl.BlockSpec(memory_space=pltpu.VMEM),
        ],
        out_specs=pl.BlockSpec(memory_space=pltpu.VMEM),
        scratch_shapes=[
            pltpu.VMEM((4, STEPS, FINE, FINE, BLOCK), BF16),
            pltpu.VMEM((4, PARTS, BLOCKS, BLOCK), BF16),
            pltpu.VMEM((3, PARTS, BLOCKS, BLOCK), F32),
        ],
        compiler_params=pltpu.CompilerParams(vmem_limit_bytes=16 * 1024 * 1024),
    )(r, arrived)


VMEM = pl.BlockSpec(memory_space=pltpu.VMEM)
SMALL = pltpu.CompilerParams(vmem_limit_bytes=4 * 1024 * 1024)
RING = 16
PLANES = 8


def source_kernel(x_ref, gate_ref, up_ref, filter_ref, out_ref):
    x = x_ref[...].astype(F32)
    mixed = up_ref[...].astype(F32) * gate_ref[...].astype(F32)
    filters = jnp.concatenate([filter_ref[i] for i in range(4)] * 2, axis=0)
    line = 0
    for value in (x[:RING], x[RING:], mixed[:RING], mixed[RING:], filters):
        for half in range(2):
            out_ref[:, line] = value[:, 128 * half : 128 * half + 128]
            line += 1
    out_ref[:, line:] = jnp.zeros((RING, 16 - line, 128), F32)


def source(x, gate, up, filters):
    return pl.pallas_call(
        source_kernel,
        out_shape=jax.ShapeDtypeStruct((RING, 16, 128), F32),
        in_specs=[VMEM] * 4,
        out_specs=VMEM,
        compiler_params=SMALL,
    )(x, gate, up, filters)


def spread_kernel(in_ref, out_ref):
    lines = [in_ref[:, line] for line in range(10)]
    for plane in range(PLANES):
        member = plane % 2
        chosen = (2 * member, 2 * member + 1, 4 + 2 * member, 5 + 2 * member, 8, 9)
        for place, line in enumerate(chosen):
            out_ref[plane, place] = lines[line]


def spread(ring):
    return pl.pallas_call(
        spread_kernel,
        out_shape=jax.ShapeDtypeStruct((PLANES, 6, RING, 128), F32),
        in_specs=[VMEM],
        out_specs=VMEM,
        compiler_params=SMALL,
    )(ring)


def exact_dot(value, pick):
    high = value.astype(BF16)
    rest = value - high.astype(F32)
    mid = rest.astype(BF16)
    low = (rest - mid.astype(F32)).astype(BF16)
    total = jnp.dot(high, pick, preferred_element_type=F32)
    total = total + jnp.dot(mid, pick, preferred_element_type=F32)
    return total + jnp.dot(low, pick, preferred_element_type=F32)


def quarter_pick(quarter, width):
    source = lax.broadcasted_iota(jnp.int32, (128, width), 0)
    target = lax.broadcasted_iota(jnp.int32, (128, width), 1)
    place = (source // FINE) * (BLOCK // PARTS) + FINE * quarter + source % FINE
    return (place == target).astype(BF16)


def sums_kernel(b_ref, out_ref):
    for quarter in range(QUARTERS):
        rows = b_ref[pl.ds(64 * quarter + 1, 32, stride=2), :]
        total = rows.reshape(4, 8, 128).sum(axis=0)
        for owner in range(4):
            out_ref[owner, 2 * quarter : 2 * quarter + 2] = total[2 * owner : 2 * owner + 2]


def sums(returned):
    return pl.pallas_call(
        sums_kernel,
        out_shape=jax.ShapeDtypeStruct((4, 8, 128), F32),
        in_specs=[VMEM],
        out_specs=VMEM,
        compiler_params=SMALL,
    )(returned)


def taps_kernel(b_ref, gf_ref):
    taps = jnp.zeros((2, BLOCK), F32)
    cross = (b_ref[0] + b_ref[1]) + (b_ref[2] + b_ref[3])
    for quarter in range(QUARTERS):
        taps = taps + exact_dot(cross[2 * quarter : 2 * quarter + 2], quarter_pick(quarter, BLOCK))
    gf_ref[...] = taps * (1.0 / math.sqrt(BLOCKS * BLOCK))


def final_taps(parts):
    return pl.pallas_call(
        taps_kernel,
        out_shape=jax.ShapeDtypeStruct((2, BLOCK), F32),
        in_specs=[VMEM],
        out_specs=VMEM,
        compiler_params=SMALL,
    )(parts)


def final_kernel(b_ref, x_ref, gate_ref, up_ref, skip_ref, gi_ref, gg_ref):
    both = jnp.zeros((32, 2 * BLOCK), F32)
    for quarter in range(QUARTERS):
        rows = b_ref[pl.ds(64 * quarter, 32, stride=2), :]
        both = both + exact_dot(rows, quarter_pick(quarter, 2 * BLOCK))
    x = x_ref[...].astype(F32)
    up = up_ref[...].astype(F32)
    mixed = up * gate_ref[...].astype(F32)
    skip = skip_ref[...]
    gg_ref[...] = (up * (both[:, :BLOCK] + skip * x)).astype(BF16)
    gi_ref[...] = (both[:, BLOCK:] + skip * mixed).astype(BF16)


def final(returned, x, gate, up, skip):
    piece = jax.ShapeDtypeStruct((32, BLOCK), BF16)
    return pl.pallas_call(
        final_kernel,
        out_shape=(piece, piece),
        in_specs=[VMEM] * 5,
        out_specs=[VMEM] * 2,
        compiler_params=SMALL,
    )(returned, x, gate, up, skip)


def exchange(rows):
    flat = rows.reshape(BLOCKS, 1, -1)
    flat = lax.all_to_all(flat, "seq", split_axis=0, concat_axis=0, tiled=True)
    return flat.reshape(rows.shape)


def body(inputs, gate_values, filters, skip_weight, grad_out):
    quarter = (lax.axis_index("seq") >> 5).astype(jnp.int32).reshape(1)
    every_filter = lax.all_gather(filters, "chan", axis=0)
    rings = [[RING * plane + z for z in range(RING)] for plane in range(PLANES)]
    planes = [[RING * plane + z for plane in range(PLANES)] for z in range(RING)]
    leaving = source(inputs, gate_values, grad_out, every_filter)
    ring = lax.all_to_all(
        leaving, "seq", split_axis=0, concat_axis=0, tiled=True, axis_index_groups=rings
    )
    arrived = lax.all_to_all(
        spread(ring), "seq", split_axis=0, concat_axis=0, tiled=True, axis_index_groups=planes
    )
    results = middle(arrived, quarter)
    returned = exchange(results)
    shares = lax.all_to_all(sums(returned), "chan", split_axis=0, concat_axis=0, tiled=True)
    grad_input, grad_gate = final(
        returned, inputs, gate_values, grad_out, skip_weight[:, None]
    )
    return (grad_input, grad_gate, final_taps(shares))


def solution(mesh):
    placed = (P("chan", "seq"), P("chan", "seq"), P("chan", "seq"), P("chan"), P("chan", "seq"))
    return jax.shard_map(
        body,
        mesh=mesh,
        in_specs=placed,
        out_specs=(P("chan", "seq"), P("chan", "seq"), P("chan", "seq")),
        check_vma=False,
    )
```

```python
import math

import jax
import jax.numpy as jnp
from jax import lax
from jax.experimental import pallas as pl
from jax.experimental.pallas import tpu as pltpu
from jax.sharding import PartitionSpec as P

BLOCK = 256
BLOCKS = 128
QUARTERS = 4
FINE = 16
PARTS = BLOCK // (QUARTERS * FINE)
STEPS = BLOCKS // FINE
F32 = jnp.float32
BF16 = jnp.bfloat16


def split(value):
    high = value.astype(BF16)
    return high, (value - high.astype(F32)).astype(BF16)


def rows_down(value):
    row = lax.broadcasted_iota(jnp.int32, value.shape, 0)
    return jnp.where(row == 0, 0.0, pltpu.roll(value, 1, 0))


def rows_up(value):
    row = lax.broadcasted_iota(jnp.int32, value.shape, 0)
    return jnp.where(row == BLOCKS - 1, 0.0, pltpu.roll(value, BLOCKS - 1, 0))


def nt_dot(left, right):
    return lax.dot_general(
        left, right, (((1,), (1,)), ((), ())), preferred_element_type=F32
    )


def window_rows(wide, start, store):
    turned = pltpu.roll(wide, (2 * BLOCK - start) % (2 * BLOCK), 1)
    half = pltpu.roll(turned, 2 * BLOCK - BLOCK // PARTS, 1)
    store(0, turned[:, :BLOCK])
    store(1, half[:, :BLOCK])
    store(2, turned[:, 128 : 128 + BLOCK])
    store(3, half[:, 128 : 128 + BLOCK])


def middle_kernel(r_ref, a_ref, out_ref, taps, windows, acc):
    r = r_ref[0]

    def signal(first):
        halves = [a_ref[pl.ds(first + half, BLOCKS, stride=6), :] for half in range(2)]
        return jnp.concatenate(halves, axis=1)

    x, g, h = signal(0), signal(2), signal(4)
    h_down = rows_down(h)

    def keep(slot):
        def store(i, rows):
            high, low = split(rows)
            windows[slot, i] = high
            windows[slot + 1, i] = low

        return store

    window_rows(jnp.concatenate([g, rows_up(g)], axis=1), FINE * r, keep(0))
    window_rows(jnp.concatenate([h_down, h], axis=1), FINE * r + FINE, keep(2))

    def taps_of(slot, wide, shift_of, low_slot=None):
        for n in range(FINE):
            turned = pltpu.roll(wide, shift_of(n) % 384, 1) if shift_of(n) % 384 else wide
            value = turned[:, 128:]
            high, low = split(value)
            taps[slot, :, n] = high.reshape(STEPS, FINE, BLOCK)
            if low_slot is not None:
                taps[low_slot, :, n] = low.reshape(STEPS, FINE, BLOCK)

    x_down = rows_down(x)
    taps_of(0, jnp.concatenate([h_down[:, 128:], h], axis=1), lambda n: n, 1)
    taps_of(2, jnp.concatenate([x_down[:, 128:], x], axis=1), lambda n: n)
    lane = lax.broadcasted_iota(jnp.int32, (BLOCK, BLOCK), 1)
    row = lax.broadcasted_iota(jnp.int32, (BLOCK, BLOCK), 0)
    mirror = (lane + row == BLOCK - 1).astype(BF16)
    flipped = jnp.dot(x.astype(BF16), mirror, preferred_element_type=F32)
    flipped_down = rows_down(flipped)
    wide = jnp.concatenate([flipped, flipped_down[:, :128]], axis=1)
    taps_of(3, pltpu.roll(wide, 128, 1), lambda n: n - (FINE - 1))

    for step in range(STEPS):
        shift = FINE * step
        size = BLOCKS - shift

        def rhs(slot):
            return taps[slot, step].reshape(BLOCK, BLOCK)

        def lhs(slot, start):
            return windows[slot, :, start : start + size].reshape(PARTS * size, BLOCK)

        g_high, g_low = lhs(0, shift), lhs(1, shift)
        h_high, h_low = lhs(2, 0), lhs(3, 0)
        cross = nt_dot(g_high, rhs(2)) + nt_dot(g_low, rhs(2))
        pulled = nt_dot(g_high, rhs(0)) + nt_dot(g_low, rhs(0)) + nt_dot(g_high, rhs(1))
        conv = nt_dot(h_high, rhs(3)) + nt_dot(h_low, rhs(3))
        for slot, start, value in ((0, shift, conv), (1, 0, pulled), (2, 0, cross)):
            value = value.reshape(PARTS, size, BLOCK)
            if step == 0:
                acc[slot] = value
            else:
                acc[slot, :, start : start + size] = acc[slot, :, start : start + size] + value

    column = lax.broadcasted_iota(jnp.int32, (BLOCKS, BLOCK), 1) % FINE
    line = lax.broadcasted_iota(jnp.int32, (BLOCKS, BLOCK), 0)
    source = lax.broadcasted_iota(jnp.int32, (BLOCK, 128), 0)
    target = lax.broadcasted_iota(jnp.int32, (BLOCK, 128), 1)
    totals = [jnp.zeros((BLOCKS, 128), F32), jnp.zeros((BLOCKS, 128), F32)]
    for slot, page, offset in ((0, 0, 0), (1, 0, 64), (2, 1, 0)):
        total = totals[page]
        for i in range(PARTS):
            value = acc[slot, i]
            for bit in (1, 2, 4, 8):
                if slot == 0:
                    moved = jnp.where(line < bit, 0.0, pltpu.roll(value, bit, 0))
                else:
                    moved = jnp.where(line >= BLOCKS - bit, 0.0, pltpu.roll(value, BLOCKS - bit, 0))
                value = jnp.where((column & bit) != 0, moved, value)
            pick = (source // FINE + FINE * i + offset == target).astype(BF16)
            high, low = split(value)
            total = total + jnp.dot(high, pick, preferred_element_type=F32)
            total = total + jnp.dot(low, pick, preferred_element_type=F32)
        totals[page] = total
    out_ref[pl.ds(0, BLOCKS, stride=2), :] = totals[0]
    out_ref[pl.ds(1, BLOCKS, stride=2), :] = totals[1]


def middle(arrived, r):
    return pl.pallas_call(
        middle_kernel,
        out_shape=jax.ShapeDtypeStruct((2 * BLOCKS, 128), F32),
        in_specs=[
            pl.BlockSpec(memory_space=pltpu.SMEM),
            pl.BlockSpec(memory_space=pltpu.VMEM),
        ],
        out_specs=pl.BlockSpec(memory_space=pltpu.VMEM),
        scratch_shapes=[
            pltpu.VMEM((4, STEPS, FINE, FINE, BLOCK), BF16),
            pltpu.VMEM((4, PARTS, BLOCKS, BLOCK), BF16),
            pltpu.VMEM((3, PARTS, BLOCKS, BLOCK), F32),
        ],
        compiler_params=pltpu.CompilerParams(vmem_limit_bytes=16 * 1024 * 1024),
    )(r, arrived)


VMEM = pl.BlockSpec(memory_space=pltpu.VMEM)
SMALL = pltpu.CompilerParams(vmem_limit_bytes=4 * 1024 * 1024)
MEMBERS = 32


def source_kernel(signal_ref, filter_ref, out_ref):
    filters = jnp.concatenate([filter_ref[i] for i in range(4)] * 4, axis=0)
    line = 0
    for value in (signal_ref[:MEMBERS], signal_ref[MEMBERS:], filters):
        for half in range(2):
            part = value[:, 128 * half : 128 * half + 128]
            out_ref[pl.ds(line, MEMBERS, stride=6), :] = part
            line += 1


def source(signals, filters):
    return pl.pallas_call(
        source_kernel,
        out_shape=jax.ShapeDtypeStruct((6 * MEMBERS, 128), F32),
        in_specs=[VMEM] * 2,
        out_specs=VMEM,
        compiler_params=SMALL,
    )(signals, filters)


def exact_dot(value, pick):
    high = value.astype(BF16)
    rest = value - high.astype(F32)
    mid = rest.astype(BF16)
    low = (rest - mid.astype(F32)).astype(BF16)
    total = jnp.dot(high, pick, preferred_element_type=F32)
    total = total + jnp.dot(mid, pick, preferred_element_type=F32)
    return total + jnp.dot(low, pick, preferred_element_type=F32)


def quarter_pick(quarter, width):
    source = lax.broadcasted_iota(jnp.int32, (128, width), 0)
    target = lax.broadcasted_iota(jnp.int32, (128, width), 1)
    place = (source // FINE) * (BLOCK // PARTS) + FINE * quarter + source % FINE
    return (place == target).astype(BF16)


def sums_kernel(b_ref, out_ref):
    for quarter in range(QUARTERS):
        rows = b_ref[pl.ds(64 * quarter + 1, 32, stride=2), :]
        total = rows.reshape(4, 8, 128).sum(axis=0)
        for owner in range(4):
            out_ref[owner, 2 * quarter : 2 * quarter + 2] = total[2 * owner : 2 * owner + 2]


def sums(returned):
    return pl.pallas_call(
        sums_kernel,
        out_shape=jax.ShapeDtypeStruct((4, 8, 128), F32),
        in_specs=[VMEM],
        out_specs=VMEM,
        compiler_params=SMALL,
    )(returned)


def taps_kernel(b_ref, gf_ref):
    taps = jnp.zeros((2, BLOCK), F32)
    cross = (b_ref[0] + b_ref[1]) + (b_ref[2] + b_ref[3])
    for quarter in range(QUARTERS):
        taps = taps + exact_dot(cross[2 * quarter : 2 * quarter + 2], quarter_pick(quarter, BLOCK))
    gf_ref[...] = taps * (1.0 / math.sqrt(BLOCKS * BLOCK))


def final_taps(parts):
    return pl.pallas_call(
        taps_kernel,
        out_shape=jax.ShapeDtypeStruct((2, BLOCK), F32),
        in_specs=[VMEM],
        out_specs=VMEM,
        compiler_params=SMALL,
    )(parts)


def final_kernel(b_ref, x_ref, gate_ref, up_ref, skip_ref, gi_ref, gg_ref):
    both = jnp.zeros((32, 2 * BLOCK), F32)
    for quarter in range(QUARTERS):
        rows = b_ref[pl.ds(64 * quarter, 32, stride=2), :]
        both = both + exact_dot(rows, quarter_pick(quarter, 2 * BLOCK))
    x = x_ref[...].astype(F32)
    up = up_ref[...].astype(F32)
    mixed = up * gate_ref[...].astype(F32)
    skip = skip_ref[...]
    gg_ref[...] = (up * (both[:, :BLOCK] + skip * x)).astype(BF16)
    gi_ref[...] = (both[:, BLOCK:] + skip * mixed).astype(BF16)


def final(returned, x, gate, up, skip):
    piece = jax.ShapeDtypeStruct((32, BLOCK), BF16)
    return pl.pallas_call(
        final_kernel,
        out_shape=(piece, piece),
        in_specs=[VMEM] * 5,
        out_specs=[VMEM] * 2,
        compiler_params=SMALL,
    )(returned, x, gate, up, skip)


def exchange(rows, groups):
    flat = rows.reshape(len(groups[0]), 1, -1)
    flat = lax.all_to_all(
        flat, "seq", split_axis=0, concat_axis=0, tiled=True, axis_index_groups=groups
    )
    return flat.reshape(rows.shape)


def body(inputs, gate_values, filters, skip_weight, grad_out):
    quarter = (lax.axis_index("seq") >> 5).astype(jnp.int32).reshape(1)
    every_filter = lax.all_gather(filters, "chan", axis=0)
    mixed = grad_out.astype(F32) * gate_values.astype(F32)
    signals = jnp.concatenate([inputs.astype(F32), mixed], axis=0)
    leaving = source(signals, every_filter)
    everyone = [list(range(BLOCKS))]
    planes = [[MEMBERS * y + w for w in range(MEMBERS)] for y in range(QUARTERS)]
    columns = [[MEMBERS * y + w for y in range(QUARTERS)] for w in range(MEMBERS)]
    segment = exchange(leaving, planes)
    copies = jnp.concatenate([segment] * QUARTERS, axis=0)
    results = middle(exchange(copies, columns), quarter)
    returned = exchange(results, everyone)
    shares = lax.all_to_all(sums(returned), "chan", split_axis=0, concat_axis=0, tiled=True)
    grad_input, grad_gate = final(
        returned, inputs, gate_values, grad_out, skip_weight[:, None]
    )
    return (grad_input, grad_gate, final_taps(shares))


def solution(mesh):
    placed = (P("chan", "seq"), P("chan", "seq"), P("chan", "seq"), P("chan"), P("chan", "seq"))
    return jax.shard_map(
        body,
        mesh=mesh,
        in_specs=placed,
        out_specs=(P("chan", "seq"), P("chan", "seq"), P("chan", "seq")),
        check_vma=False,
    )
```

```python
import math

import jax
import jax.numpy as jnp
from jax import lax
from jax.experimental import pallas as pl
from jax.experimental.pallas import tpu as pltpu
from jax.sharding import PartitionSpec as P

BLOCK = 256
BLOCKS = 128
QUARTERS = 4
FINE = 16
PARTS = BLOCK // (QUARTERS * FINE)
STEPS = BLOCKS // FINE
F32 = jnp.float32
BF16 = jnp.bfloat16


def split(value):
    high = value.astype(BF16)
    return high, (value - high.astype(F32)).astype(BF16)


def rows_down(value):
    row = lax.broadcasted_iota(jnp.int32, value.shape, 0)
    return jnp.where(row == 0, 0.0, pltpu.roll(value, 1, 0))


def rows_up(value):
    row = lax.broadcasted_iota(jnp.int32, value.shape, 0)
    return jnp.where(row == BLOCKS - 1, 0.0, pltpu.roll(value, BLOCKS - 1, 0))


def nt_dot(left, right):
    return lax.dot_general(
        left, right, (((1,), (1,)), ((), ())), preferred_element_type=F32
    )


def window_rows(wide, start, store):
    turned = pltpu.roll(wide, (2 * BLOCK - start) % (2 * BLOCK), 1)
    half = pltpu.roll(turned, 2 * BLOCK - BLOCK // PARTS, 1)
    store(0, turned[:, :BLOCK])
    store(1, half[:, :BLOCK])
    store(2, turned[:, 128 : 128 + BLOCK])
    store(3, half[:, 128 : 128 + BLOCK])


def middle_kernel(r_ref, a_ref, out_ref, taps, windows, acc):
    r = r_ref[0]

    lane = lax.broadcasted_iota(jnp.int32, (MEMBERS, 128), 1) < 64

    def join(even, odd):
        first = jnp.where(lane, even, pltpu.roll(odd, 64, 1))
        return first, jnp.where(lane, pltpu.roll(even, 64, 1), odd)

    rows_x, rows_g, rows_h = [], [], []
    for y in range(QUARTERS):
        tiles_x, tiles_g, tiles_h = [], [], []
        for part in (0, 2):
            even, odd = 4 * y + part, 4 * y + part + 1
            tile_x, tile_g = join(a_ref[even, :MEMBERS], a_ref[odd, :MEMBERS])
            tile_h = jnp.where(
                lane[:16], a_ref[even, MEMBERS:], pltpu.roll(a_ref[odd, MEMBERS:], 64, 1)
            )
            tile_i = jnp.where(
                lane[:16], pltpu.roll(a_ref[even, MEMBERS:], 64, 1), a_ref[odd, MEMBERS:]
            )
            tiles_x.append(tile_x)
            tiles_g.append(tile_g)
            tiles_h.append(jnp.concatenate([tile_h, tile_i], axis=0))
        rows_x.append(jnp.concatenate(tiles_x, axis=1))
        rows_g.append(jnp.concatenate(tiles_g, axis=1))
        rows_h.append(jnp.concatenate(tiles_h, axis=1))
    x = jnp.concatenate(rows_x, axis=0)
    g = jnp.concatenate(rows_g, axis=0)
    h = jnp.concatenate(rows_h, axis=0)
    h_down = rows_down(h)

    def keep(slot):
        def store(i, rows):
            high, low = split(rows)
            windows[slot, i] = high
            windows[slot + 1, i] = low

        return store

    window_rows(jnp.concatenate([g, rows_up(g)], axis=1), FINE * r, keep(0))
    window_rows(jnp.concatenate([h_down, h], axis=1), FINE * r + FINE, keep(2))

    def taps_of(slot, wide, shift_of, low_slot=None):
        for n in range(FINE):
            turned = pltpu.roll(wide, shift_of(n) % 384, 1) if shift_of(n) % 384 else wide
            value = turned[:, 128:]
            high, low = split(value)
            taps[slot, :, n] = high.reshape(STEPS, FINE, BLOCK)
            if low_slot is not None:
                taps[low_slot, :, n] = low.reshape(STEPS, FINE, BLOCK)

    x_down = rows_down(x)
    taps_of(0, jnp.concatenate([h_down[:, 128:], h], axis=1), lambda n: n, 1)
    taps_of(2, jnp.concatenate([x_down[:, 128:], x], axis=1), lambda n: n)
    ahead = lax.broadcasted_iota(jnp.int32, (BLOCK, BLOCK), 1)
    below = lax.broadcasted_iota(jnp.int32, (BLOCK, BLOCK), 0)
    mirror = (ahead + below == BLOCK - 1).astype(BF16)
    flipped = jnp.dot(x.astype(BF16), mirror, preferred_element_type=F32)
    flipped_down = rows_down(flipped)
    wide = jnp.concatenate([flipped, flipped_down[:, :128]], axis=1)
    taps_of(3, pltpu.roll(wide, 128, 1), lambda n: n - (FINE - 1))

    for step in range(STEPS):
        shift = FINE * step
        size = BLOCKS - shift

        def rhs(slot):
            return taps[slot, step].reshape(BLOCK, BLOCK)

        def lhs(slot, start):
            return windows[slot, :, start : start + size].reshape(PARTS * size, BLOCK)

        g_high, g_low = lhs(0, shift), lhs(1, shift)
        h_high, h_low = lhs(2, 0), lhs(3, 0)
        cross = nt_dot(g_high, rhs(2)) + nt_dot(g_low, rhs(2))
        pulled = nt_dot(g_high, rhs(0)) + nt_dot(g_low, rhs(0)) + nt_dot(g_high, rhs(1))
        conv = nt_dot(h_high, rhs(3)) + nt_dot(h_low, rhs(3))
        for slot, start, value in ((0, shift, conv), (1, 0, pulled), (2, 0, cross)):
            value = value.reshape(PARTS, size, BLOCK)
            if step == 0:
                acc[slot] = value
            else:
                acc[slot, :, start : start + size] = acc[slot, :, start : start + size] + value

    column = lax.broadcasted_iota(jnp.int32, (BLOCKS, BLOCK), 1) % FINE
    line = lax.broadcasted_iota(jnp.int32, (BLOCKS, BLOCK), 0)
    source = lax.broadcasted_iota(jnp.int32, (BLOCK, 128), 0)
    target = lax.broadcasted_iota(jnp.int32, (BLOCK, 128), 1)
    totals = [jnp.zeros((BLOCKS, 128), F32), jnp.zeros((BLOCKS, 128), F32)]
    for slot, page, offset in ((0, 0, 0), (1, 0, 64), (2, 1, 0)):
        total = totals[page]
        for i in range(PARTS):
            value = acc[slot, i]
            for bit in (1, 2, 4, 8):
                if slot == 0:
                    moved = jnp.where(line < bit, 0.0, pltpu.roll(value, bit, 0))
                else:
                    moved = jnp.where(line >= BLOCKS - bit, 0.0, pltpu.roll(value, BLOCKS - bit, 0))
                value = jnp.where((column & bit) != 0, moved, value)
            pick = (source // FINE + FINE * i + offset == target).astype(BF16)
            high, low = split(value)
            total = total + jnp.dot(high, pick, preferred_element_type=F32)
            total = total + jnp.dot(low, pick, preferred_element_type=F32)
        totals[page] = total
    out_ref[pl.ds(0, BLOCKS, stride=2), :] = totals[0]
    out_ref[pl.ds(1, BLOCKS, stride=2), :] = totals[1]


def middle(arrived, r):
    return pl.pallas_call(
        middle_kernel,
        out_shape=jax.ShapeDtypeStruct((2 * BLOCKS, 128), F32),
        in_specs=[
            pl.BlockSpec(memory_space=pltpu.SMEM),
            pl.BlockSpec(memory_space=pltpu.VMEM),
        ],
        out_specs=pl.BlockSpec(memory_space=pltpu.VMEM),
        scratch_shapes=[
            pltpu.VMEM((4, STEPS, FINE, FINE, BLOCK), BF16),
            pltpu.VMEM((4, PARTS, BLOCKS, BLOCK), BF16),
            pltpu.VMEM((3, PARTS, BLOCKS, BLOCK), F32),
        ],
        compiler_params=pltpu.CompilerParams(vmem_limit_bytes=16 * 1024 * 1024),
    )(r, arrived)


VMEM = pl.BlockSpec(memory_space=pltpu.VMEM)
SMALL = pltpu.CompilerParams(vmem_limit_bytes=4 * 1024 * 1024)
MEMBERS = 32


def source_kernel(signal_ref, out_ref):
    lane = lax.broadcasted_iota(jnp.int32, (MEMBERS, 128), 1) < 64
    x, g = signal_ref[:MEMBERS], signal_ref[MEMBERS : 2 * MEMBERS]
    h = jnp.concatenate([signal_ref[2 * MEMBERS :]] * 4, axis=0)
    for part in range(4):
        at = 128 * (part // 2)
        px, pg, ph = x[:, at : at + 128], g[:, at : at + 128], h[:, at : at + 128]
        if part % 2 == 0:
            pg = pltpu.roll(pg, 64, 1)
        else:
            px, ph = pltpu.roll(px, 64, 1), pltpu.roll(ph, 64, 1)
        out_ref[pl.ds(2 * part, MEMBERS, stride=8), :] = jnp.where(lane, px, pg)
        out_ref[pl.ds(2 * part + 1, MEMBERS, stride=8), :] = ph


def source(signals):
    return pl.pallas_call(
        source_kernel,
        out_shape=jax.ShapeDtypeStruct((8 * MEMBERS, 128), F32),
        in_specs=[VMEM],
        out_specs=VMEM,
        compiler_params=SMALL,
    )(signals)


def spread_kernel(owner_ref, in_ref, out_ref):
    owner = owner_ref[0]
    taps = in_ref[pl.ds(1, MEMBERS, stride=8), :]
    for slot in range(1, 4):
        taps = jnp.where(owner == slot, in_ref[pl.ds(2 * slot + 1, MEMBERS, stride=8), :], taps)
    lane = lax.broadcasted_iota(jnp.int32, (16, 128), 1) < 64
    packed = jnp.where(lane, taps[:16], pltpu.roll(taps[16:], 64, 1))
    for slot in range(4):
        tokens = in_ref[pl.ds(2 * slot, MEMBERS, stride=8), :]
        for y in range(QUARTERS):
            out_ref[4 * y + slot, :MEMBERS] = tokens
            out_ref[4 * y + slot, MEMBERS:] = packed


def spread(owner, segment):
    return pl.pallas_call(
        spread_kernel,
        out_shape=jax.ShapeDtypeStruct((16, 48, 128), F32),
        in_specs=[pl.BlockSpec(memory_space=pltpu.SMEM), VMEM],
        out_specs=VMEM,
        compiler_params=SMALL,
    )(owner, segment)


def exact_dot(value, pick):
    high = value.astype(BF16)
    rest = value - high.astype(F32)
    mid = rest.astype(BF16)
    low = (rest - mid.astype(F32)).astype(BF16)
    total = jnp.dot(high, pick, preferred_element_type=F32)
    total = total + jnp.dot(mid, pick, preferred_element_type=F32)
    return total + jnp.dot(low, pick, preferred_element_type=F32)


def quarter_pick(quarter, width):
    source = lax.broadcasted_iota(jnp.int32, (128, width), 0)
    target = lax.broadcasted_iota(jnp.int32, (128, width), 1)
    place = (source // FINE) * (BLOCK // PARTS) + FINE * quarter + source % FINE
    return (place == target).astype(BF16)


def sums_kernel(b_ref, out_ref):
    for quarter in range(QUARTERS):
        rows = b_ref[pl.ds(64 * quarter + 1, 32, stride=2), :]
        total = rows.reshape(4, 8, 128).sum(axis=0)
        for owner in range(4):
            out_ref[owner, 2 * quarter : 2 * quarter + 2] = total[2 * owner : 2 * owner + 2]


def sums(returned):
    return pl.pallas_call(
        sums_kernel,
        out_shape=jax.ShapeDtypeStruct((4, 8, 128), F32),
        in_specs=[VMEM],
        out_specs=VMEM,
        compiler_params=SMALL,
    )(returned)


def taps_kernel(b_ref, gf_ref):
    taps = jnp.zeros((2, BLOCK), F32)
    cross = (b_ref[0] + b_ref[1]) + (b_ref[2] + b_ref[3])
    for quarter in range(QUARTERS):
        taps = taps + exact_dot(cross[2 * quarter : 2 * quarter + 2], quarter_pick(quarter, BLOCK))
    gf_ref[...] = taps * (1.0 / math.sqrt(BLOCKS * BLOCK))


def final_taps(parts):
    return pl.pallas_call(
        taps_kernel,
        out_shape=jax.ShapeDtypeStruct((2, BLOCK), F32),
        in_specs=[VMEM],
        out_specs=VMEM,
        compiler_params=SMALL,
    )(parts)


def final_kernel(b_ref, x_ref, gate_ref, up_ref, skip_ref, gi_ref, gg_ref):
    both = jnp.zeros((32, 2 * BLOCK), F32)
    for quarter in range(QUARTERS):
        rows = b_ref[pl.ds(64 * quarter, 32, stride=2), :]
        both = both + exact_dot(rows, quarter_pick(quarter, 2 * BLOCK))
    x = x_ref[...].astype(F32)
    up = up_ref[...].astype(F32)
    mixed = up * gate_ref[...].astype(F32)
    skip = skip_ref[...]
    gg_ref[...] = (up * (both[:, :BLOCK] + skip * x)).astype(BF16)
    gi_ref[...] = (both[:, BLOCK:] + skip * mixed).astype(BF16)


def final(returned, x, gate, up, skip):
    piece = jax.ShapeDtypeStruct((32, BLOCK), BF16)
    return pl.pallas_call(
        final_kernel,
        out_shape=(piece, piece),
        in_specs=[VMEM] * 5,
        out_specs=[VMEM] * 2,
        compiler_params=SMALL,
    )(returned, x, gate, up, skip)


def exchange(rows, groups):
    flat = rows.reshape(len(groups[0]), 1, -1)
    flat = lax.all_to_all(
        flat, ("seq", "chan"), split_axis=0, concat_axis=0, tiled=True, axis_index_groups=groups
    )
    return flat.reshape(rows.shape)


def body(inputs, gate_values, filters, skip_weight, grad_out):
    def device(y, w, slot):
        return 4 * (MEMBERS * y + w) + slot

    planes = [
        [device(y, w, slot) for w in range(MEMBERS) for slot in range(4)]
        for y in range(QUARTERS)
    ]
    columns = [
        [device(y, w, slot) for y in range(QUARTERS) for slot in range(4)]
        for w in range(MEMBERS)
    ]
    slots = [
        [device(y, w, slot) for y in range(QUARTERS) for w in range(MEMBERS)]
        for slot in range(4)
    ]
    place = lax.axis_index("seq").astype(jnp.int32)
    quarter = (place >> 5).reshape(1)
    owner = ((place >> 1) & 3).reshape(1)
    mixed = grad_out.astype(F32) * gate_values.astype(F32)
    pairs = jnp.concatenate([filters] * 4, axis=0)
    signals = jnp.concatenate([inputs.astype(F32), mixed, pairs], axis=0)
    signals, quarter, owner = lax.optimization_barrier((signals, quarter, owner))
    segment = exchange(source(signals), planes)
    results = middle(exchange(spread(owner, segment), columns), quarter)
    returned = exchange(results, slots)
    shares = lax.all_to_all(sums(returned), "chan", split_axis=0, concat_axis=0, tiled=True)
    grad_input, grad_gate = final(
        returned, inputs, gate_values, grad_out, skip_weight[:, None]
    )
    return (grad_input, grad_gate, final_taps(shares))


def solution(mesh):
    placed = (P("chan", "seq"), P("chan", "seq"), P("chan", "seq"), P("chan"), P("chan", "seq"))
    return jax.shard_map(
        body,
        mesh=mesh,
        in_specs=placed,
        out_specs=(P("chan", "seq"), P("chan", "seq"), P("chan", "seq")),
        check_vma=False,
    )
```

```python
import math

import jax
import jax.numpy as jnp
from jax import lax
from jax.experimental import pallas as pl
from jax.experimental.pallas import tpu as pltpu
from jax.sharding import PartitionSpec as P

BLOCK = 256
BLOCKS = 128
QUARTERS = 4
FINE = 16
PARTS = BLOCK // (QUARTERS * FINE)
STEPS = BLOCKS // FINE
F32 = jnp.float32
BF16 = jnp.bfloat16


def split(value):
    high = value.astype(BF16)
    return high, (value - high.astype(F32)).astype(BF16)


def rows_down(value):
    row = lax.broadcasted_iota(jnp.int32, value.shape, 0)
    return jnp.where(row == 0, 0.0, pltpu.roll(value, 1, 0))


def rows_up(value):
    row = lax.broadcasted_iota(jnp.int32, value.shape, 0)
    return jnp.where(row == BLOCKS - 1, 0.0, pltpu.roll(value, BLOCKS - 1, 0))


def nt_dot(left, right):
    return lax.dot_general(
        left, right, (((1,), (1,)), ((), ())), preferred_element_type=F32
    )


def window_rows(wide, start, store):
    turned = pltpu.roll(wide, (2 * BLOCK - start) % (2 * BLOCK), 1)
    half = pltpu.roll(turned, 2 * BLOCK - BLOCK // PARTS, 1)
    store(0, turned[:, :BLOCK])
    store(1, half[:, :BLOCK])
    store(2, turned[:, 128 : 128 + BLOCK])
    store(3, half[:, 128 : 128 + BLOCK])


def middle_kernel(r_ref, a_ref, out_ref, taps, windows, acc):
    r = r_ref[0]

    def signal(first):
        halves = [a_ref[pl.ds(first + half, BLOCKS, stride=6), :] for half in range(2)]
        return jnp.concatenate(halves, axis=1)

    x, g, h = signal(0), signal(2), signal(4)
    h_down = rows_down(h)

    def keep(slot):
        def store(i, rows):
            high, low = split(rows)
            windows[slot, i] = high
            windows[slot + 1, i] = low

        return store

    window_rows(jnp.concatenate([g, rows_up(g)], axis=1), FINE * r, keep(0))
    window_rows(jnp.concatenate([h_down, h], axis=1), FINE * r + FINE, keep(2))

    def taps_of(slot, wide, shift_of, low_slot=None):
        for n in range(FINE):
            turned = pltpu.roll(wide, shift_of(n) % 384, 1) if shift_of(n) % 384 else wide
            value = turned[:, 128:]
            high, low = split(value)
            taps[slot, :, n] = high.reshape(STEPS, FINE, BLOCK)
            if low_slot is not None:
                taps[low_slot, :, n] = low.reshape(STEPS, FINE, BLOCK)

    def products(slot, left, right, down, extra=None):
        for step in range(STEPS):
            shift = FINE * step
            size = BLOCKS - shift
            begin, start = (0, shift) if down else (shift, 0)
            both = windows[left : left + 2, :, begin : begin + size]
            both = both.reshape(2 * PARTS * size, BLOCK)
            value = nt_dot(both, taps[right, step].reshape(BLOCK, BLOCK))
            value = value[: PARTS * size] + value[PARTS * size :]
            if extra is not None:
                high = both[: PARTS * size]
                value = value + nt_dot(high, taps[extra, step].reshape(BLOCK, BLOCK))
            value = value.reshape(PARTS, size, BLOCK)
            if step == 0:
                acc[slot] = value
            else:
                acc[slot, :, start : start + size] = acc[slot, :, start : start + size] + value

    column = lax.broadcasted_iota(jnp.int32, (BLOCKS, BLOCK), 1) % FINE
    line = lax.broadcasted_iota(jnp.int32, (BLOCKS, BLOCK), 0)
    source = lax.broadcasted_iota(jnp.int32, (BLOCK, 128), 0)
    target = lax.broadcasted_iota(jnp.int32, (BLOCK, 128), 1)

    def collected(slot, down, offset):
        total = jnp.zeros((BLOCKS, 128), F32)
        for i in range(PARTS):
            value = acc[slot, i]
            for bit in (1, 2, 4, 8):
                if down:
                    moved = jnp.where(line < bit, 0.0, pltpu.roll(value, bit, 0))
                else:
                    moved = jnp.where(line >= BLOCKS - bit, 0.0, pltpu.roll(value, BLOCKS - bit, 0))
                value = jnp.where((column & bit) != 0, moved, value)
            pick = (source // FINE + FINE * i + offset == target).astype(BF16)
            high, low = split(value)
            total = total + jnp.dot(high, pick, preferred_element_type=F32)
            total = total + jnp.dot(low, pick, preferred_element_type=F32)
        return total

    x_down = rows_down(x)
    lane = lax.broadcasted_iota(jnp.int32, (BLOCK, BLOCK), 1)
    row = lax.broadcasted_iota(jnp.int32, (BLOCK, BLOCK), 0)
    mirror = (lane + row == BLOCK - 1).astype(BF16)
    flipped = jnp.dot(x.astype(BF16), mirror, preferred_element_type=F32)
    flipped_down = rows_down(flipped)
    wide = jnp.concatenate([flipped, flipped_down[:, :128]], axis=1)
    taps_of(3, pltpu.roll(wide, 128, 1), lambda n: n - (FINE - 1))

    taps_of(0, jnp.concatenate([h_down[:, 128:], h], axis=1), lambda n: n, 1)
    taps_of(2, jnp.concatenate([x_down[:, 128:], x], axis=1), lambda n: n)
    products(0, 2, 3, True)
    products(1, 0, 0, False, extra=1)
    products(2, 0, 2, False)
    conv = collected(0, True, 0)
    pulled = collected(1, False, 64)
    cross = collected(2, False, 0)
    out_ref[pl.ds(0, BLOCKS, stride=2), :] = conv + pulled
    out_ref[pl.ds(1, BLOCKS, stride=2), :] = cross


def middle(arrived, r):
    return pl.pallas_call(
        middle_kernel,
        out_shape=jax.ShapeDtypeStruct((2 * BLOCKS, 128), F32),
        in_specs=[
            pl.BlockSpec(memory_space=pltpu.SMEM),
            pl.BlockSpec(memory_space=pltpu.VMEM),
        ],
        out_specs=pl.BlockSpec(memory_space=pltpu.VMEM),
        scratch_shapes=[
            pltpu.VMEM((4, STEPS, FINE, FINE, BLOCK), BF16),
            pltpu.VMEM((4, PARTS, BLOCKS, BLOCK), BF16),
            pltpu.VMEM((3, PARTS, BLOCKS, BLOCK), F32),
        ],
        compiler_params=pltpu.CompilerParams(vmem_limit_bytes=16 * 1024 * 1024),
    )(r, arrived)


VMEM = pl.BlockSpec(memory_space=pltpu.VMEM)
SMALL = pltpu.CompilerParams(vmem_limit_bytes=4 * 1024 * 1024)
MEMBERS = 32


def source_kernel(signal_ref, filter_ref, out_ref):
    filters = jnp.concatenate([filter_ref[i] for i in range(4)] * 4, axis=0)
    line = 0
    for value in (signal_ref[:MEMBERS], signal_ref[MEMBERS:], filters):
        for half in range(2):
            part = value[:, 128 * half : 128 * half + 128]
            for quarter in range(QUARTERS):
                start = 6 * MEMBERS * quarter + line
                out_ref[pl.ds(start, MEMBERS, stride=6), :] = part
            line += 1


def source(signals, filters):
    return pl.pallas_call(
        source_kernel,
        out_shape=jax.ShapeDtypeStruct((6 * BLOCKS, 128), F32),
        in_specs=[VMEM] * 2,
        out_specs=VMEM,
        compiler_params=SMALL,
    )(signals, filters)


def exact_dot(value, pick):
    high = value.astype(BF16)
    rest = value - high.astype(F32)
    mid = rest.astype(BF16)
    low = (rest - mid.astype(F32)).astype(BF16)
    total = jnp.dot(high, pick, preferred_element_type=F32)
    total = total + jnp.dot(mid, pick, preferred_element_type=F32)
    return total + jnp.dot(low, pick, preferred_element_type=F32)


def quarter_pick(quarter, width):
    source = lax.broadcasted_iota(jnp.int32, (128, width), 0)
    target = lax.broadcasted_iota(jnp.int32, (128, width), 1)
    place = (source // FINE) * (BLOCK // PARTS) + FINE * quarter + source % FINE
    return (place == target).astype(BF16)


def sums_kernel(b_ref, out_ref):
    for quarter in range(QUARTERS):
        rows = b_ref[pl.ds(64 * quarter + 1, 32, stride=2), :]
        total = rows.reshape(4, 8, 128).sum(axis=0)
        for owner in range(4):
            out_ref[owner, 2 * quarter : 2 * quarter + 2] = total[2 * owner : 2 * owner + 2]


def sums(returned):
    return pl.pallas_call(
        sums_kernel,
        out_shape=jax.ShapeDtypeStruct((4, 8, 128), F32),
        in_specs=[VMEM],
        out_specs=VMEM,
        compiler_params=SMALL,
    )(returned)


def taps_kernel(b_ref, gf_ref):
    taps = jnp.zeros((2, BLOCK), F32)
    cross = (b_ref[0] + b_ref[1]) + (b_ref[2] + b_ref[3])
    for quarter in range(QUARTERS):
        taps = taps + exact_dot(cross[2 * quarter : 2 * quarter + 2], quarter_pick(quarter, BLOCK))
    gf_ref[...] = taps * (1.0 / math.sqrt(BLOCKS * BLOCK))


def final_taps(parts):
    return pl.pallas_call(
        taps_kernel,
        out_shape=jax.ShapeDtypeStruct((2, BLOCK), F32),
        in_specs=[VMEM],
        out_specs=VMEM,
        compiler_params=SMALL,
    )(parts)


def final_kernel(b_ref, x_ref, gate_ref, up_ref, skip_ref, gi_ref, gg_ref):
    both = jnp.zeros((32, 2 * BLOCK), F32)
    for quarter in range(QUARTERS):
        rows = b_ref[pl.ds(64 * quarter, 32, stride=2), :]
        both = both + exact_dot(rows, quarter_pick(quarter, 2 * BLOCK))
    x = x_ref[...].astype(F32)
    up = up_ref[...].astype(F32)
    mixed = up * gate_ref[...].astype(F32)
    skip = skip_ref[...]
    gg_ref[...] = (up * (both[:, :BLOCK] + skip * x)).astype(BF16)
    gi_ref[...] = (both[:, BLOCK:] + skip * mixed).astype(BF16)


def final(returned, x, gate, up, skip):
    piece = jax.ShapeDtypeStruct((32, BLOCK), BF16)
    return pl.pallas_call(
        final_kernel,
        out_shape=(piece, piece),
        in_specs=[VMEM] * 5,
        out_specs=[VMEM] * 2,
        compiler_params=SMALL,
    )(returned, x, gate, up, skip)


def exchange(rows):
    flat = rows.reshape(BLOCKS, 1, -1)
    flat = lax.all_to_all(flat, "seq", split_axis=0, concat_axis=0, tiled=True)
    return flat.reshape(rows.shape)


def body(inputs, gate_values, filters, skip_weight, grad_out):
    quarter = (lax.axis_index("seq") >> 5).astype(jnp.int32).reshape(1)
    mixed = grad_out.astype(F32) * gate_values.astype(F32)
    signals = jnp.concatenate([inputs.astype(F32), mixed], axis=0)
    every_filter = lax.all_gather(filters, "chan", axis=0)
    signals, quarter = lax.optimization_barrier((signals, quarter))
    results = middle(exchange(source(signals, every_filter)), quarter)
    returned = exchange(results)
    shares = lax.all_to_all(sums(returned), "chan", split_axis=0, concat_axis=0, tiled=True)
    grad_input, grad_gate = final(
        returned, inputs, gate_values, grad_out, skip_weight[:, None]
    )
    return (grad_input, grad_gate, final_taps(shares))


def solution(mesh):
    placed = (P("chan", "seq"), P("chan", "seq"), P("chan", "seq"), P("chan"), P("chan", "seq"))
    return jax.shard_map(
        body,
        mesh=mesh,
        in_specs=placed,
        out_specs=(P("chan", "seq"), P("chan", "seq"), P("chan", "seq")),
        check_vma=False,
    )
```

```python
import math

import jax
import jax.numpy as jnp
from jax import lax
from jax.experimental import pallas as pl
from jax.experimental.pallas import tpu as pltpu
from jax.sharding import PartitionSpec as P

BLOCK = 256
BLOCKS = 128
QUARTERS = 4
FINE = 16
PARTS = BLOCK // (QUARTERS * FINE)
STEPS = BLOCKS // FINE
F32 = jnp.float32
BF16 = jnp.bfloat16


def split(value):
    high = value.astype(BF16)
    return high, (value - high.astype(F32)).astype(BF16)


def rows_down(value):
    row = lax.broadcasted_iota(jnp.int32, value.shape, 0)
    return jnp.where(row == 0, 0.0, pltpu.roll(value, 1, 0))


def rows_up(value):
    row = lax.broadcasted_iota(jnp.int32, value.shape, 0)
    return jnp.where(row == BLOCKS - 1, 0.0, pltpu.roll(value, BLOCKS - 1, 0))


def nt_dot(left, right):
    return lax.dot_general(
        left, right, (((1,), (1,)), ((), ())), preferred_element_type=F32
    )


def window_rows(wide, start, store):
    turned = pltpu.roll(wide, (2 * BLOCK - start) % (2 * BLOCK), 1)
    half = pltpu.roll(turned, 2 * BLOCK - BLOCK // PARTS, 1)
    store(0, turned[:, :BLOCK])
    store(1, half[:, :BLOCK])
    store(2, turned[:, 128 : 128 + BLOCK])
    store(3, half[:, 128 : 128 + BLOCK])


def middle_kernel(r_ref, a_ref, out_ref, taps, windows, acc):
    r = r_ref[0]

    def signal(first):
        halves = [a_ref[:, first + half].reshape(BLOCKS, 128) for half in range(2)]
        return jnp.concatenate(halves, axis=1)

    x, g, h = signal(0), signal(2), signal(4)
    h_down = rows_down(h)

    def keep(slot):
        def store(i, rows):
            high, low = split(rows)
            windows[slot, i] = high
            windows[slot + 1, i] = low

        return store

    window_rows(jnp.concatenate([g, rows_up(g)], axis=1), FINE * r, keep(0))
    window_rows(jnp.concatenate([h_down, h], axis=1), FINE * r + FINE, keep(2))

    def taps_of(slot, wide, shift_of, low_slot=None):
        for n in range(FINE):
            turned = pltpu.roll(wide, shift_of(n) % 384, 1) if shift_of(n) % 384 else wide
            value = turned[:, 128:]
            high, low = split(value)
            taps[slot, :, n] = high.reshape(STEPS, FINE, BLOCK)
            if low_slot is not None:
                taps[low_slot, :, n] = low.reshape(STEPS, FINE, BLOCK)

    def products(slot, left, right, down, extra=None):
        for step in range(STEPS):
            shift = FINE * step
            size = BLOCKS - shift
            begin, start = (0, shift) if down else (shift, 0)
            both = windows[left : left + 2, :, begin : begin + size]
            both = both.reshape(2 * PARTS * size, BLOCK)
            value = nt_dot(both, taps[right, step].reshape(BLOCK, BLOCK))
            value = value[: PARTS * size] + value[PARTS * size :]
            if extra is not None:
                high = both[: PARTS * size]
                value = value + nt_dot(high, taps[extra, step].reshape(BLOCK, BLOCK))
            value = value.reshape(PARTS, size, BLOCK)
            if step == 0:
                acc[slot] = value
            else:
                acc[slot, :, start : start + size] = acc[slot, :, start : start + size] + value

    column = lax.broadcasted_iota(jnp.int32, (BLOCKS, BLOCK), 1) % FINE
    line = lax.broadcasted_iota(jnp.int32, (BLOCKS, BLOCK), 0)
    source = lax.broadcasted_iota(jnp.int32, (BLOCK, 128), 0)
    target = lax.broadcasted_iota(jnp.int32, (BLOCK, 128), 1)

    def collected(slot, down, offset):
        total = jnp.zeros((BLOCKS, 128), F32)
        for i in range(PARTS):
            value = acc[slot, i]
            for bit in (1, 2, 4, 8):
                if down:
                    moved = jnp.where(line < bit, 0.0, pltpu.roll(value, bit, 0))
                else:
                    moved = jnp.where(line >= BLOCKS - bit, 0.0, pltpu.roll(value, BLOCKS - bit, 0))
                value = jnp.where((column & bit) != 0, moved, value)
            pick = (source // FINE + FINE * i + offset == target).astype(BF16)
            high, low = split(value)
            total = total + jnp.dot(high, pick, preferred_element_type=F32)
            total = total + jnp.dot(low, pick, preferred_element_type=F32)
        return total

    x_down = rows_down(x)
    lane = lax.broadcasted_iota(jnp.int32, (BLOCK, BLOCK), 1)
    row = lax.broadcasted_iota(jnp.int32, (BLOCK, BLOCK), 0)
    mirror = (lane + row == BLOCK - 1).astype(BF16)
    flipped = jnp.dot(x.astype(BF16), mirror, preferred_element_type=F32)
    flipped_down = rows_down(flipped)
    wide = jnp.concatenate([flipped, flipped_down[:, :128]], axis=1)
    taps_of(3, pltpu.roll(wide, 128, 1), lambda n: n - (FINE - 1))

    taps_of(0, jnp.concatenate([h_down[:, 128:], h], axis=1), lambda n: n, 1)
    taps_of(2, jnp.concatenate([x_down[:, 128:], x], axis=1), lambda n: n)
    products(0, 2, 3, True)
    products(1, 0, 0, False, extra=1)
    products(2, 0, 2, False)
    conv = collected(0, True, 0)
    pulled = collected(1, False, 64)
    cross = collected(2, False, 0)
    out_ref[pl.ds(0, BLOCKS, stride=2), :] = conv + pulled
    out_ref[pl.ds(1, BLOCKS, stride=2), :] = cross


def middle(arrived, r):
    return pl.pallas_call(
        middle_kernel,
        out_shape=jax.ShapeDtypeStruct((2 * BLOCKS, 128), F32),
        in_specs=[
            pl.BlockSpec(memory_space=pltpu.SMEM),
            pl.BlockSpec(memory_space=pltpu.VMEM),
        ],
        out_specs=pl.BlockSpec(memory_space=pltpu.VMEM),
        scratch_shapes=[
            pltpu.VMEM((4, STEPS, FINE, FINE, BLOCK), BF16),
            pltpu.VMEM((4, PARTS, BLOCKS, BLOCK), BF16),
            pltpu.VMEM((3, PARTS, BLOCKS, BLOCK), F32),
        ],
        compiler_params=pltpu.CompilerParams(vmem_limit_bytes=16 * 1024 * 1024),
    )(r, arrived)


VMEM = pl.BlockSpec(memory_space=pltpu.VMEM)
SMALL = pltpu.CompilerParams(vmem_limit_bytes=4 * 1024 * 1024)
RING = 16
PLANES = 8


def source_kernel(signal_ref, filter_ref, skip_ref, out_ref, aside_ref):
    filters = jnp.concatenate([filter_ref[i] for i in range(4)] * 2, axis=0)
    line = 0
    for value in [signal_ref[RING * i : RING * i + RING] for i in range(4)] + [filters]:
        for half in range(2):
            part = value[:, 128 * half : 128 * half + 128]
            out_ref[pl.ds(line, RING, stride=10), :] = part
            line += 1
    across = lax.broadcasted_iota(jnp.int32, (32, 32), 1)
    down = lax.broadcasted_iota(jnp.int32, (32, 32), 0)
    skip = jnp.where(across == down, skip_ref[...], 0.0).sum(axis=1, keepdims=True)
    aside_ref[...] = jnp.broadcast_to(skip, aside_ref.shape)


def source(signals, filters, skip):
    return pl.pallas_call(
        source_kernel,
        out_shape=(
            jax.ShapeDtypeStruct((10 * RING, 128), F32),
            jax.ShapeDtypeStruct((32, BLOCK), F32),
        ),
        in_specs=[VMEM] * 3,
        out_specs=[VMEM] * 2,
        compiler_params=SMALL,
    )(signals, filters, skip)


def spread_kernel(in_ref, out_ref):
    lines = [in_ref[pl.ds(line, RING, stride=10), :] for line in range(10)]
    for plane in range(PLANES):
        member = plane % 2
        chosen = (2 * member, 2 * member + 1, 4 + 2 * member, 5 + 2 * member, 8, 9)
        for place, line in enumerate(chosen):
            out_ref[plane, place] = lines[line]


def spread(ring):
    return pl.pallas_call(
        spread_kernel,
        out_shape=jax.ShapeDtypeStruct((PLANES, 6, RING, 128), F32),
        in_specs=[VMEM],
        out_specs=VMEM,
        compiler_params=SMALL,
    )(ring)


def exact_dot(value, pick):
    high = value.astype(BF16)
    rest = value - high.astype(F32)
    mid = rest.astype(BF16)
    low = (rest - mid.astype(F32)).astype(BF16)
    total = jnp.dot(high, pick, preferred_element_type=F32)
    total = total + jnp.dot(mid, pick, preferred_element_type=F32)
    return total + jnp.dot(low, pick, preferred_element_type=F32)


def quarter_pick(quarter, width):
    source = lax.broadcasted_iota(jnp.int32, (128, width), 0)
    target = lax.broadcasted_iota(jnp.int32, (128, width), 1)
    place = (source // FINE) * (BLOCK // PARTS) + FINE * quarter + source % FINE
    return (place == target).astype(BF16)


def sums_kernel(b_ref, out_ref):
    lane = lax.broadcasted_iota(jnp.int32, (8, 128), 1) < 64
    totals = []
    for quarter in range(QUARTERS):
        rows = b_ref[pl.ds(64 * quarter + 1, 32, stride=2), :]
        totals.append(rows.reshape(4, 8, 128).sum(axis=0))
    for k in range(2):
        out_ref[k] = jnp.where(lane, totals[2 * k], pltpu.roll(totals[2 * k + 1], 64, 1))


def sums(returned):
    return pl.pallas_call(
        sums_kernel,
        out_shape=jax.ShapeDtypeStruct((2, 8, 128), F32),
        in_specs=[VMEM],
        out_specs=VMEM,
        compiler_params=SMALL,
    )(returned)


def final_kernel(slot_ref, b_ref, signal_ref, up_ref, skip_ref, shares_ref, gi_ref, gg_ref, gf_ref):
    both = jnp.zeros((32, 2 * BLOCK), F32)
    for quarter in range(QUARTERS):
        rows = b_ref[pl.ds(64 * quarter, 32, stride=2), :]
        both = both + exact_dot(rows, quarter_pick(quarter, 2 * BLOCK))
    x, mixed = signal_ref[:32], signal_ref[32:]
    up, skip = up_ref[...].astype(F32), skip_ref[...]
    gg_ref[...] = (up * (both[:, :BLOCK] + skip * x)).astype(BF16)
    gi_ref[...] = (both[:, BLOCK:] + skip * mixed).astype(BF16)

    source = lax.broadcasted_iota(jnp.int32, (128, BLOCK), 0)
    target = lax.broadcasted_iota(jnp.int32, (128, BLOCK), 1)
    taps = jnp.zeros((8, BLOCK), F32)
    for k in range(2):
        total = (shares_ref[0, k] + shares_ref[1, k]) + (shares_ref[2, k] + shares_ref[3, k])
        token = source % 64
        place = (token // FINE) * (BLOCK // PARTS) + FINE * (2 * k + source // 64) + token % FINE
        taps = taps + exact_dot(total, (place == target).astype(BF16))
    slot = slot_ref[0]
    own = taps[:2]
    for other in range(1, 4):
        own = jnp.where(slot == other, taps[2 * other : 2 * other + 2], own)
    gf_ref[...] = own * (1.0 / math.sqrt(BLOCKS * BLOCK))


def final(slot, returned, signals, upstream, skip, shares):
    piece = jax.ShapeDtypeStruct((32, BLOCK), BF16)
    return pl.pallas_call(
        final_kernel,
        out_shape=(piece, piece, jax.ShapeDtypeStruct((2, BLOCK), F32)),
        in_specs=[pl.BlockSpec(memory_space=pltpu.SMEM)] + [VMEM] * 5,
        out_specs=[VMEM] * 3,
        compiler_params=SMALL,
    )(slot, returned, signals, upstream, skip, shares)


def exchange(rows, groups=None):
    members = BLOCKS if groups is None else len(groups[0])
    flat = lax.all_to_all(
        rows.reshape(members, 1, -1),
        "seq",
        split_axis=0,
        concat_axis=0,
        tiled=True,
        axis_index_groups=groups,
    )
    return flat.reshape(rows.shape)


def body(inputs, gate_values, filters, skip_weight, grad_out):
    rings = [[RING * plane + z for z in range(RING)] for plane in range(PLANES)]
    planes = [[RING * plane + z for plane in range(PLANES)] for z in range(RING)]
    mixed = grad_out.astype(F32) * gate_values.astype(F32)
    signals = jnp.concatenate([inputs.astype(F32), mixed], axis=0)
    every_filter = lax.all_gather(filters, "chan", axis=0)
    leaving, skip = source(signals, every_filter, skip_weight[None, :])
    quarter = (lax.axis_index("seq") >> 5).astype(jnp.int32).reshape(1)
    slot = lax.axis_index("chan").astype(jnp.int32).reshape(1)
    leaving, quarter, slot = lax.optimization_barrier((leaving, quarter, slot))
    arrived = exchange(spread(exchange(leaving, rings)), planes)
    returned = exchange(middle(arrived, quarter))
    shares = lax.all_gather(sums(returned), "chan", axis=0)
    return final(slot, returned, signals, grad_out, skip, shares)


def solution(mesh):
    placed = (P("chan", "seq"), P("chan", "seq"), P("chan", "seq"), P("chan"), P("chan", "seq"))
    return jax.shard_map(
        body,
        mesh=mesh,
        in_specs=placed,
        out_specs=(P("chan", "seq"), P("chan", "seq"), P("chan", "seq")),
        check_vma=False,
    )
```

```python
import functools
import math

import jax
import jax.numpy as jnp
from jax import lax
from jax.experimental import pallas as pl
from jax.experimental.pallas import tpu as pltpu
from jax.sharding import PartitionSpec as P

BLOCK = 256
BLOCKS = 128
FINE = 16
PARTS = BLOCK // FINE
RING = 16
PLANES = 8
F32 = jnp.float32
BF16 = jnp.bfloat16


def split(value):
    high = value.astype(BF16)
    return high, (value - high.astype(F32)).astype(BF16)


def rows_down(value):
    row = lax.broadcasted_iota(jnp.int32, value.shape, 0)
    return jnp.where(row == 0, 0.0, pltpu.roll(value, 1, 0))


def rows_up(value):
    row = lax.broadcasted_iota(jnp.int32, value.shape, 0)
    return jnp.where(row == BLOCKS - 1, 0.0, pltpu.roll(value, BLOCKS - 1, 0))


def nt_dot(left, right):
    return lax.dot_general(
        left, right, (((1,), (1,)), ((), ())), preferred_element_type=F32
    )


def middle_kernel(plane_ref, a_ref, out_ref, h_wide, x_wide, f_wide, g_ext, x_ext, taps, ahead, behind, acc):
    plane = plane_ref[0]

    def signal(first):
        halves = [a_ref[:, first + half].reshape(BLOCKS, 128) for half in range(2)]
        return jnp.concatenate(halves, axis=1)

    def runs(value):
        return value.reshape(PLANES, RING, value.shape[1])

    h = signal(8)
    h_down = rows_down(h)
    across = lax.broadcasted_iota(jnp.int32, (BLOCK, BLOCK), 1)
    down = lax.broadcasted_iota(jnp.int32, (BLOCK, BLOCK), 0)
    mirror = (across + down == BLOCK - 1).astype(BF16)
    for place, piece in enumerate(split(h)):
        flipped = jnp.dot(piece, mirror, preferred_element_type=F32)
        wide = jnp.concatenate([rows_down(flipped)[:, :128], flipped], axis=1)
        f_wide[place] = runs(wide.astype(BF16))
    for place, piece in enumerate(split(jnp.concatenate([h_down[:, 128:], h], axis=1))):
        h_wide[place] = runs(piece)
    for member in range(2):
        x = signal(2 * member)
        g = signal(4 + 2 * member)
        x_down = rows_down(x)
        x_wide[member] = runs(jnp.concatenate([x_down[:, 128:], x], axis=1).astype(BF16))
        x_ext[member] = runs(jnp.concatenate([x_down, x], axis=1).astype(BF16))
        for place, piece in enumerate(split(jnp.concatenate([g, rows_up(g)], axis=1))):
            g_ext[member, place] = runs(piece)

    def turn(value, shift):
        size = value.shape[1]
        return pltpu.roll(value, shift % size, 1) if shift % size else value

    def taps_of(slot, wide, step, least):
        for n in range(FINE):
            taps[slot, step, n] = turn(wide, least + n)[:, 128:]

    def ahead_taps(step):
        for place in range(2):
            taps_of(place, h_wide[place, step], step, 0)
            taps_of(2 + place, x_wide[place, step], step, 0)

    def behind_taps(step):
        for place in range(2):
            taps_of(4 + place, f_wide[place, step], step, 1 - FINE)

    size = PARTS * RING

    def rhs(slot, step):
        return taps[slot, step].reshape(BLOCK, BLOCK)

    def pulled_and_cross(lhs, step):
        high = nt_dot(lhs, rhs(0, step))
        pulled, cross = [], None
        for member in range(2):
            at = 2 * size * member
            low = nt_dot(lhs[at : at + size], rhs(1, step))
            pulled.append(high[at : at + size] + high[at + size : at + 2 * size] + low)
            both = nt_dot(lhs[at : at + 2 * size], rhs(2 + member, step))
            both = both[:size] + both[size:]
            cross = both if cross is None else cross + both
        return pulled[0], pulled[1], cross

    def convolved(lhs, step):
        both = nt_dot(lhs, rhs(4, step)) + nt_dot(lhs, rhs(5, step))
        return both[:size], both[size:]

    def ahead_step(step):
        for member in range(2):
            for place in range(2):
                wide = g_ext[member, place, plane + step]
                for i in range(PARTS):
                    ahead[member, place, i] = turn(wide, -FINE * i)[:, :BLOCK]
        lhs = ahead[...].reshape(4 * size, BLOCK)
        if step:
            for k, value in enumerate(pulled_and_cross(lhs, step - 1)):
                acc[1, 2 + k] += value
        for k, value in enumerate(pulled_and_cross(lhs, step)):
            if step:
                acc[0, 2 + k] += value
            else:
                acc[0, 2 + k] = value
                acc[1, 2 + k] = jnp.zeros((size, BLOCK), F32)
        if step + 1 < PLANES:
            ahead_taps(step + 1)

    def behind_step(step):
        for member in range(2):
            wide = x_ext[member, plane - step]
            for i in range(PARTS):
                behind[member, i] = turn(wide, -FINE * (i + 1))[:, :BLOCK]
        lhs = behind[...].reshape(2 * size, BLOCK)
        if step:
            for k, value in enumerate(convolved(lhs, step - 1)):
                acc[1, k] += value
        for k, value in enumerate(convolved(lhs, step)):
            if step:
                acc[0, k] += value
            else:
                acc[0, k] = value
                acc[1, k] = jnp.zeros((size, BLOCK), F32)
        if step + 1 < PLANES:
            behind_taps(step + 1)

    ahead_taps(0)
    behind_taps(0)
    ahead_step(0)
    behind_step(0)
    for step in range(1, PLANES):
        pl.when(step < PLANES - plane)(functools.partial(ahead_step, step))
    for step in range(1, PLANES):
        pl.when(step <= plane)(functools.partial(behind_step, step))

    lanes = lax.broadcasted_iota(jnp.int32, (RING, BLOCK), 1) % FINE
    lines = lax.broadcasted_iota(jnp.int32, (RING, BLOCK), 0)
    source = lax.broadcasted_iota(jnp.int32, (BLOCK, BLOCK), 0) // FINE
    target = lax.broadcasted_iota(jnp.int32, (BLOCK, BLOCK), 1)
    total = jnp.zeros((5 * RING, BLOCK), F32)
    for i in range(PARTS):
        pieces = []
        for k in range(5):
            near = acc[0, k, RING * i : RING * i + RING]
            far = acc[1, k, RING * i : RING * i + RING]
            value = jnp.where(lines + lanes < RING if k < 2 else lines >= lanes, near, far)
            for bit in (1, 2, 4, 8):
                moved = pltpu.roll(value, bit if k < 2 else RING - bit, 0)
                value = jnp.where((lanes & bit) != 0, moved, value)
            pieces.append(value)
        pick = (source + FINE * i == target).astype(BF16)
        high, low = split(jnp.concatenate(pieces, axis=0))
        total = total + jnp.dot(high, pick, preferred_element_type=F32)
        total = total + jnp.dot(low, pick, preferred_element_type=F32)
    for k in range(5):
        for half in range(2):
            part = total[RING * k : RING * k + RING, 128 * half : 128 * half + 128]
            out_ref[pl.ds(2 * k + half, RING, stride=10), :] = part


def middle(arrived, plane):
    return pl.pallas_call(
        middle_kernel,
        out_shape=jax.ShapeDtypeStruct((10 * RING, 128), F32),
        in_specs=[
            pl.BlockSpec(memory_space=pltpu.SMEM),
            pl.BlockSpec(memory_space=pltpu.VMEM),
        ],
        out_specs=pl.BlockSpec(memory_space=pltpu.VMEM),
        scratch_shapes=[
            pltpu.VMEM((2, PLANES, RING, 384), BF16),
            pltpu.VMEM((2, PLANES, RING, 384), BF16),
            pltpu.VMEM((2, PLANES, RING, 384), BF16),
            pltpu.VMEM((2, 2, PLANES, RING, 2 * BLOCK), BF16),
            pltpu.VMEM((2, PLANES, RING, 2 * BLOCK), BF16),
            pltpu.VMEM((6, PLANES, FINE, FINE, BLOCK), BF16),
            pltpu.VMEM((2, 2, PARTS, RING, BLOCK), BF16),
            pltpu.VMEM((2, PARTS, RING, BLOCK), BF16),
            pltpu.VMEM((2, 5, PARTS * RING, BLOCK), F32),
        ],
        compiler_params=pltpu.CompilerParams(vmem_limit_bytes=32 * 1024 * 1024),
    )(plane, arrived)


VMEM = pl.BlockSpec(memory_space=pltpu.VMEM)
SMALL = pltpu.CompilerParams(vmem_limit_bytes=4 * 1024 * 1024)


def source_kernel(signal_ref, filter_ref, skip_ref, out_ref, aside_ref):
    filters = jnp.concatenate([filter_ref[i] for i in range(4)] * 2, axis=0)
    line = 0
    for value in [signal_ref[RING * i : RING * i + RING] for i in range(4)] + [filters]:
        for half in range(2):
            part = value[:, 128 * half : 128 * half + 128]
            out_ref[pl.ds(line, RING, stride=10), :] = part
            line += 1
    across = lax.broadcasted_iota(jnp.int32, (32, 32), 1)
    down = lax.broadcasted_iota(jnp.int32, (32, 32), 0)
    skip = jnp.where(across == down, skip_ref[...], 0.0).sum(axis=1, keepdims=True)
    aside_ref[...] = jnp.broadcast_to(skip, aside_ref.shape)


def source(signals, filters, skip):
    return pl.pallas_call(
        source_kernel,
        out_shape=(
            jax.ShapeDtypeStruct((10 * RING, 128), F32),
            jax.ShapeDtypeStruct((32, BLOCK), F32),
        ),
        in_specs=[VMEM] * 3,
        out_specs=[VMEM] * 2,
        compiler_params=SMALL,
    )(signals, filters, skip)


def spread_kernel(in_ref, out_ref):
    for line in range(10):
        rows = in_ref[pl.ds(line, RING, stride=10), :]
        for plane in range(PLANES):
            out_ref[plane, line] = rows


def spread(ring):
    return pl.pallas_call(
        spread_kernel,
        out_shape=jax.ShapeDtypeStruct((PLANES, 10, RING, 128), F32),
        in_specs=[VMEM],
        out_specs=VMEM,
        compiler_params=SMALL,
    )(ring)


def sums_kernel(b_ref, out_ref):
    for half in range(2):
        rows = b_ref[pl.ds(8 + half, RING, stride=10), :]
        out_ref[:, 128 * half : 128 * half + 128] = rows[:8] + rows[8:]


def sums(returned):
    return pl.pallas_call(
        sums_kernel,
        out_shape=jax.ShapeDtypeStruct((8, BLOCK), F32),
        in_specs=[VMEM],
        out_specs=VMEM,
        compiler_params=SMALL,
    )(returned)


def final_kernel(slot_ref, b_ref, signal_ref, up_ref, skip_ref, shares_ref, gi_ref, gg_ref, gf_ref):
    def channels(first):
        halves = [
            jnp.concatenate(
                [b_ref[pl.ds(first + 2 * member + half, RING, stride=10), :] for member in range(2)],
                axis=0,
            )
            for half in range(2)
        ]
        return jnp.concatenate(halves, axis=1)

    x, mixed = signal_ref[:32], signal_ref[32:]
    up, skip = up_ref[...].astype(F32), skip_ref[...]
    gg_ref[...] = (up * (channels(0) + skip * x)).astype(BF16)
    gi_ref[...] = (channels(4) + skip * mixed).astype(BF16)
    taps = (shares_ref[0] + shares_ref[1]) + (shares_ref[2] + shares_ref[3])
    slot = slot_ref[0]
    own = taps[:2]
    for other in range(1, 4):
        own = jnp.where(slot == other, taps[2 * other : 2 * other + 2], own)
    gf_ref[...] = own * (1.0 / math.sqrt(BLOCKS * BLOCK))


def final(slot, returned, signals, upstream, skip, shares):
    piece = jax.ShapeDtypeStruct((32, BLOCK), BF16)
    return pl.pallas_call(
        final_kernel,
        out_shape=(piece, piece, jax.ShapeDtypeStruct((2, BLOCK), F32)),
        in_specs=[pl.BlockSpec(memory_space=pltpu.SMEM)] + [VMEM] * 5,
        out_specs=[VMEM] * 3,
        compiler_params=SMALL,
    )(slot, returned, signals, upstream, skip, shares)


def exchange(rows, groups=None):
    members = BLOCKS if groups is None else len(groups[0])
    flat = lax.all_to_all(
        rows.reshape(members, 1, -1),
        "seq",
        split_axis=0,
        concat_axis=0,
        tiled=True,
        axis_index_groups=groups,
    )
    return flat.reshape(rows.shape)


def body(inputs, gate_values, filters, skip_weight, grad_out):
    rings = [[RING * plane + z for z in range(RING)] for plane in range(PLANES)]
    planes = [[RING * plane + z for plane in range(PLANES)] for z in range(RING)]
    mixed = grad_out.astype(F32) * gate_values.astype(F32)
    signals = jnp.concatenate([inputs.astype(F32), mixed], axis=0)
    every_filter = lax.all_gather(filters, "chan", axis=0)
    leaving, skip = source(signals, every_filter, skip_weight[None, :])
    plane = (lax.axis_index("seq") >> 4).astype(jnp.int32).reshape(1)
    slot = lax.axis_index("chan").astype(jnp.int32).reshape(1)
    leaving, plane, slot = lax.optimization_barrier((leaving, plane, slot))
    arrived = exchange(spread(exchange(leaving, rings)), planes)
    returned = exchange(middle(arrived, plane), rings)
    shares = lax.all_gather(sums(returned), "chan", axis=0)
    return final(slot, returned, signals, grad_out, skip, shares)


def solution(mesh):
    placed = (P("chan", "seq"), P("chan", "seq"), P("chan", "seq"), P("chan"), P("chan", "seq"))
    return jax.shard_map(
        body,
        mesh=mesh,
        in_specs=placed,
        out_specs=(P("chan", "seq"), P("chan", "seq"), P("chan", "seq")),
        check_vma=False,
    )
```

```python
import functools
import math

import jax
import jax.numpy as jnp
from jax import lax
from jax.experimental import pallas as pl
from jax.experimental.pallas import tpu as pltpu
from jax.sharding import PartitionSpec as P

BLOCK = 256
BLOCKS = 128
FINE = 16
PARTS = BLOCK // FINE
RING = 16
PLANES = 8
F32 = jnp.float32
BF16 = jnp.bfloat16


def split(value):
    high = value.astype(BF16)
    return high, (value - high.astype(F32)).astype(BF16)


def rows_down(value):
    row = lax.broadcasted_iota(jnp.int32, value.shape, 0)
    return jnp.where(row == 0, 0.0, pltpu.roll(value, 1, 0))


def rows_up(value):
    row = lax.broadcasted_iota(jnp.int32, value.shape, 0)
    return jnp.where(row == BLOCKS - 1, 0.0, pltpu.roll(value, BLOCKS - 1, 0))


def nt_dot(left, right):
    return lax.dot_general(
        left, right, (((1,), (1,)), ((), ())), preferred_element_type=F32
    )


def middle_kernel(plane_ref, a_ref, out_ref, h_wide, x_wide, f_wide, g_ext, x_ext, taps, ahead, behind, acc):
    plane = plane_ref[0]

    def signal(first):
        halves = [a_ref[:, first + half].reshape(BLOCKS, 128) for half in range(2)]
        return jnp.concatenate(halves, axis=1)

    def runs(value):
        return value.reshape(PLANES, RING, value.shape[1])

    h = signal(8)
    h_down = rows_down(h)
    across = lax.broadcasted_iota(jnp.int32, (BLOCK, BLOCK), 1)
    down = lax.broadcasted_iota(jnp.int32, (BLOCK, BLOCK), 0)
    mirror = (across + down == BLOCK - 1).astype(BF16)
    for place, piece in enumerate(split(h)):
        flipped = jnp.dot(piece, mirror, preferred_element_type=F32)
        wide = jnp.concatenate([rows_down(flipped)[:, :128], flipped], axis=1)
        f_wide[place] = runs(wide.astype(BF16))
    for place, piece in enumerate(split(jnp.concatenate([h_down[:, 128:], h], axis=1))):
        h_wide[place] = runs(piece)
    for member in range(2):
        x = signal(2 * member)
        g = signal(4 + 2 * member)
        x_down = rows_down(x)
        x_wide[member] = runs(jnp.concatenate([x_down[:, 128:], x], axis=1).astype(BF16))
        x_ext[member] = runs(jnp.concatenate([x_down, x], axis=1).astype(BF16))
        for place, piece in enumerate(split(jnp.concatenate([g, rows_up(g)], axis=1))):
            g_ext[member, place] = runs(piece)

    def turn(value, shift):
        size = value.shape[1]
        return pltpu.roll(value, shift % size, 1) if shift % size else value

    def taps_of(slot, wide, step, least):
        for n in range(FINE):
            taps[slot, step, n] = turn(wide, least + n)[:, 128:]

    def ahead_taps(step):
        for place in range(2):
            taps_of(place, h_wide[place, step], step, 0)
            taps_of(2 + place, x_wide[place, step], step, 0)

    def behind_taps(step):
        for place in range(2):
            taps_of(4 + place, f_wide[place, step], step, 1 - FINE)

    size = PARTS * RING

    def rhs(slot, step):
        return taps[slot, step].reshape(BLOCK, BLOCK)

    def pulled_and_cross(lhs, step):
        high = nt_dot(lhs, rhs(0, step))
        pulled, cross = [], None
        for member in range(2):
            at = 2 * size * member
            low = nt_dot(lhs[at : at + size], rhs(1, step))
            pulled.append(high[at : at + size] + high[at + size : at + 2 * size] + low)
            both = nt_dot(lhs[at : at + 2 * size], rhs(2 + member, step))
            both = both[:size] + both[size:]
            cross = both if cross is None else cross + both
        return pulled[0], pulled[1], cross

    def convolved(lhs, step):
        both = nt_dot(lhs, rhs(4, step)) + nt_dot(lhs, rhs(5, step))
        return both[:size], both[size:]

    def ahead_step(step, first):
        for member in range(2):
            for place in range(2):
                wide = g_ext[member, place, plane + step]
                for i in range(PARTS):
                    ahead[member, place, i] = turn(wide, -FINE * i)[:, :BLOCK]
        lhs = ahead[...].reshape(4 * size, BLOCK)
        if not first:
            for k, value in enumerate(pulled_and_cross(lhs, step - 1)):
                acc[1, 2 + k] += value
        for k, value in enumerate(pulled_and_cross(lhs, step)):
            if not first:
                acc[0, 2 + k] += value
            else:
                acc[0, 2 + k] = value
                acc[1, 2 + k] = jnp.zeros((size, BLOCK), F32)
        ahead_taps(jnp.minimum(step + 1, PLANES - 1) if not first else 1)

    def behind_step(step, first):
        for member in range(2):
            wide = x_ext[member, plane - step]
            for i in range(PARTS):
                behind[member, i] = turn(wide, -FINE * (i + 1))[:, :BLOCK]
        lhs = behind[...].reshape(2 * size, BLOCK)
        if not first:
            for k, value in enumerate(convolved(lhs, step - 1)):
                acc[1, k] += value
        for k, value in enumerate(convolved(lhs, step)):
            if not first:
                acc[0, k] += value
            else:
                acc[0, k] = value
                acc[1, k] = jnp.zeros((size, BLOCK), F32)
        behind_taps(jnp.minimum(step + 1, PLANES - 1) if not first else 1)

    ahead_taps(0)
    behind_taps(0)
    ahead_step(0, True)
    behind_step(0, True)
    def ahead_loop(step, carry):
        ahead_step(step, False)
        return carry

    def behind_loop(step, carry):
        behind_step(step, False)
        return carry

    lax.fori_loop(1, PLANES - plane, ahead_loop, 0)
    lax.fori_loop(1, plane + 1, behind_loop, 0)

    lanes = lax.broadcasted_iota(jnp.int32, (RING, BLOCK), 1) % FINE
    lines = lax.broadcasted_iota(jnp.int32, (RING, BLOCK), 0)
    source = lax.broadcasted_iota(jnp.int32, (BLOCK, BLOCK), 0) // FINE
    target = lax.broadcasted_iota(jnp.int32, (BLOCK, BLOCK), 1)
    total = jnp.zeros((5 * RING, BLOCK), F32)
    for i in range(PARTS):
        pieces = []
        for k in range(5):
            near = acc[0, k, RING * i : RING * i + RING]
            far = acc[1, k, RING * i : RING * i + RING]
            value = jnp.where(lines + lanes < RING if k < 2 else lines >= lanes, near, far)
            for bit in (1, 2, 4, 8):
                moved = pltpu.roll(value, bit if k < 2 else RING - bit, 0)
                value = jnp.where((lanes & bit) != 0, moved, value)
            pieces.append(value)
        pick = (source + FINE * i == target).astype(BF16)
        both = jnp.concatenate(split(jnp.concatenate(pieces, axis=0)), axis=0)
        both = jnp.dot(both, pick, preferred_element_type=F32)
        total = total + (both[: 5 * RING] + both[5 * RING :])
    for k in range(5):
        for half in range(2):
            part = total[RING * k : RING * k + RING, 128 * half : 128 * half + 128]
            out_ref[pl.ds(2 * k + half, RING, stride=10), :] = part


def middle(arrived, plane):
    return pl.pallas_call(
        middle_kernel,
        out_shape=jax.ShapeDtypeStruct((10 * RING, 128), F32),
        in_specs=[
            pl.BlockSpec(memory_space=pltpu.SMEM),
            pl.BlockSpec(memory_space=pltpu.VMEM),
        ],
        out_specs=pl.BlockSpec(memory_space=pltpu.VMEM),
        scratch_shapes=[
            pltpu.VMEM((2, PLANES, RING, 384), BF16),
            pltpu.VMEM((2, PLANES, RING, 384), BF16),
            pltpu.VMEM((2, PLANES, RING, 384), BF16),
            pltpu.VMEM((2, 2, PLANES, RING, 2 * BLOCK), BF16),
            pltpu.VMEM((2, PLANES, RING, 2 * BLOCK), BF16),
            pltpu.VMEM((6, PLANES, FINE, FINE, BLOCK), BF16),
            pltpu.VMEM((2, 2, PARTS, RING, BLOCK), BF16),
            pltpu.VMEM((2, PARTS, RING, BLOCK), BF16),
            pltpu.VMEM((2, 5, PARTS * RING, BLOCK), F32),
        ],
        compiler_params=pltpu.CompilerParams(vmem_limit_bytes=32 * 1024 * 1024),
    )(plane, arrived)


VMEM = pl.BlockSpec(memory_space=pltpu.VMEM)
SMALL = pltpu.CompilerParams(vmem_limit_bytes=4 * 1024 * 1024)


def source_kernel(signal_ref, filter_ref, skip_ref, out_ref, aside_ref):
    filters = jnp.concatenate([filter_ref[i] for i in range(4)] * 2, axis=0)
    line = 0
    for value in [signal_ref[RING * i : RING * i + RING] for i in range(4)] + [filters]:
        for half in range(2):
            part = value[:, 128 * half : 128 * half + 128]
            out_ref[pl.ds(line, RING, stride=10), :] = part
            line += 1
    across = lax.broadcasted_iota(jnp.int32, (32, 32), 1)
    down = lax.broadcasted_iota(jnp.int32, (32, 32), 0)
    skip = jnp.where(across == down, skip_ref[...], 0.0).sum(axis=1, keepdims=True)
    aside_ref[...] = jnp.broadcast_to(skip, aside_ref.shape)


def source(signals, filters, skip):
    return pl.pallas_call(
        source_kernel,
        out_shape=(
            jax.ShapeDtypeStruct((10 * RING, 128), F32),
            jax.ShapeDtypeStruct((32, BLOCK), F32),
        ),
        in_specs=[VMEM] * 3,
        out_specs=[VMEM] * 2,
        compiler_params=SMALL,
    )(signals, filters, skip)


def spread_kernel(in_ref, out_ref):
    for line in range(10):
        rows = in_ref[pl.ds(line, RING, stride=10), :]
        for plane in range(PLANES):
            out_ref[plane, line] = rows


def spread(ring):
    return pl.pallas_call(
        spread_kernel,
        out_shape=jax.ShapeDtypeStruct((PLANES, 10, RING, 128), F32),
        in_specs=[VMEM],
        out_specs=VMEM,
        compiler_params=SMALL,
    )(ring)


def sums_kernel(b_ref, out_ref):
    for half in range(2):
        rows = b_ref[pl.ds(8 + half, RING, stride=10), :]
        out_ref[:, 128 * half : 128 * half + 128] = rows[:8] + rows[8:]


def sums(returned):
    return pl.pallas_call(
        sums_kernel,
        out_shape=jax.ShapeDtypeStruct((8, BLOCK), F32),
        in_specs=[VMEM],
        out_specs=VMEM,
        compiler_params=SMALL,
    )(returned)


def final_kernel(slot_ref, b_ref, signal_ref, up_ref, skip_ref, shares_ref, gi_ref, gg_ref, gf_ref):
    def channels(first):
        halves = [
            jnp.concatenate(
                [b_ref[pl.ds(first + 2 * member + half, RING, stride=10), :] for member in range(2)],
                axis=0,
            )
            for half in range(2)
        ]
        return jnp.concatenate(halves, axis=1)

    x, mixed = signal_ref[:32], signal_ref[32:]
    up, skip = up_ref[...].astype(F32), skip_ref[...]
    gg_ref[...] = (up * (channels(0) + skip * x)).astype(BF16)
    gi_ref[...] = (channels(4) + skip * mixed).astype(BF16)
    taps = (shares_ref[0] + shares_ref[1]) + (shares_ref[2] + shares_ref[3])
    slot = slot_ref[0]
    own = taps[:2]
    for other in range(1, 4):
        own = jnp.where(slot == other, taps[2 * other : 2 * other + 2], own)
    gf_ref[...] = own * (1.0 / math.sqrt(BLOCKS * BLOCK))


def final(slot, returned, signals, upstream, skip, shares):
    piece = jax.ShapeDtypeStruct((32, BLOCK), BF16)
    return pl.pallas_call(
        final_kernel,
        out_shape=(piece, piece, jax.ShapeDtypeStruct((2, BLOCK), F32)),
        in_specs=[pl.BlockSpec(memory_space=pltpu.SMEM)] + [VMEM] * 5,
        out_specs=[VMEM] * 3,
        compiler_params=SMALL,
    )(slot, returned, signals, upstream, skip, shares)


def exchange(rows, groups=None):
    members = BLOCKS if groups is None else len(groups[0])
    flat = lax.all_to_all(
        rows.reshape(members, 1, -1),
        "seq",
        split_axis=0,
        concat_axis=0,
        tiled=True,
        axis_index_groups=groups,
    )
    return flat.reshape(rows.shape)


def body(inputs, gate_values, filters, skip_weight, grad_out):
    rings = [[RING * plane + z for z in range(RING)] for plane in range(PLANES)]
    planes = [[RING * plane + z for plane in range(PLANES)] for z in range(RING)]
    mixed = grad_out.astype(F32) * gate_values.astype(F32)
    signals = jnp.concatenate([inputs.astype(F32), mixed], axis=0)
    every_filter = lax.all_gather(filters, "chan", axis=0)
    leaving, skip = source(signals, every_filter, skip_weight[None, :])
    plane = (lax.axis_index("seq") >> 4).astype(jnp.int32).reshape(1)
    slot = lax.axis_index("chan").astype(jnp.int32).reshape(1)
    leaving, plane, slot = lax.optimization_barrier((leaving, plane, slot))
    arrived = exchange(spread(exchange(leaving, rings)), planes)
    returned = exchange(middle(arrived, plane), rings)
    shares = lax.all_gather(sums(returned), "chan", axis=0)
    return final(slot, returned, signals, grad_out, skip, shares)


def solution(mesh):
    placed = (P("chan", "seq"), P("chan", "seq"), P("chan", "seq"), P("chan"), P("chan", "seq"))
    return jax.shard_map(
        body,
        mesh=mesh,
        in_specs=placed,
        out_specs=(P("chan", "seq"), P("chan", "seq"), P("chan", "seq")),
        check_vma=False,
    )
```

```python
import functools
import math

import jax
import jax.numpy as jnp
from jax import lax
from jax.experimental import pallas as pl
from jax.experimental.pallas import tpu as pltpu
from jax.sharding import PartitionSpec as P

BLOCK = 256
BLOCKS = 128
FINE = 16
PARTS = BLOCK // FINE
RING = 16
PLANES = 8
F32 = jnp.float32
BF16 = jnp.bfloat16


def split(value):
    high = value.astype(BF16)
    return high, (value - high.astype(F32)).astype(BF16)


def rows_down(value):
    row = lax.broadcasted_iota(jnp.int32, value.shape, 0)
    return jnp.where(row == 0, 0.0, pltpu.roll(value, 1, 0))


def rows_up(value):
    row = lax.broadcasted_iota(jnp.int32, value.shape, 0)
    return jnp.where(row == BLOCKS - 1, 0.0, pltpu.roll(value, BLOCKS - 1, 0))


def nt_dot(left, right):
    return lax.dot_general(
        left, right, (((1,), (1,)), ((), ())), preferred_element_type=F32
    )


def middle_kernel(plane_ref, a_ref, out_ref, h_wide, x_wide, f_wide, g_ext, x_ext, taps_a, taps_b, ahead, behind, acc):
    plane = plane_ref[0]

    def signal(first):
        halves = [a_ref[:, first + half].reshape(BLOCKS, 128) for half in range(2)]
        return jnp.concatenate(halves, axis=1)

    def turn(value, shift):
        size = value.shape[1]
        return pltpu.roll(value, shift % size, 1) if shift % size else value

    def pairs(value, shift):
        parts = [part.reshape(PLANES, 2, 8, -1) for part in (value, turn(value, shift))]
        return jnp.concatenate(parts, axis=2)

    h = signal(8)
    h_down = rows_down(h)
    across = lax.broadcasted_iota(jnp.int32, (BLOCK, BLOCK), 1)
    down = lax.broadcasted_iota(jnp.int32, (BLOCK, BLOCK), 0)
    mirror = (across + down == BLOCK - 1).astype(BF16)
    for place, piece in enumerate(split(h)):
        flipped = jnp.dot(piece, mirror, preferred_element_type=F32)
        wide = jnp.concatenate([rows_down(flipped)[:, :128], flipped], axis=1)
        f_wide[place] = pairs(wide, 1).astype(BF16)
    for place, piece in enumerate(split(pairs(jnp.concatenate([h_down[:, 128:], h], axis=1), 1))):
        h_wide[place] = piece
    for member in range(2):
        x = signal(2 * member)
        g = signal(4 + 2 * member)
        x_down = rows_down(x)
        x_wide[member] = pairs(jnp.concatenate([x_down[:, 128:], x], axis=1), 1).astype(BF16)
        x_ext[member] = pairs(jnp.concatenate([x_down, x], axis=1), -FINE).astype(BF16)
        wide = pairs(jnp.concatenate([g, rows_up(g)], axis=1), -FINE)
        for place, piece in enumerate(split(wide)):
            g_ext[member, place] = piece

    size = PARTS * 8

    def taps_of(ref, side, slot, wide_ref, place, step, least):
        for half in range(2):
            wide = wide_ref[place, step, half]
            for n in range(0, FINE, 2):
                ref[side, slot, half, n // 2] = turn(wide, least + n)[:, 128:]

    def tile(ref, side, slot, half):
        if half is None:
            return ref[side, slot].reshape(BLOCK, BLOCK)
        return ref[side, slot, half].reshape(128, BLOCK)

    def ahead_build(side, step):
        step = jnp.minimum(step, PLANES - 1)
        at = jnp.minimum(plane + step, PLANES - 1)
        for member in range(2):
            for place in range(2):
                for half in range(2):
                    wide = g_ext[member, place, at, half]
                    for i in range(0, PARTS, 2):
                        rows = turn(wide, -FINE * i)[:, :BLOCK]
                        ahead[side, half, member, place, i // 2] = rows
        for place in range(2):
            taps_of(taps_a, side, place, h_wide, place, step, 0)
            taps_of(taps_a, side, 2 + place, x_wide, place, step, 0)

    def behind_build(side, step):
        step = jnp.minimum(step, PLANES - 1)
        at = jnp.maximum(plane - step, 0)
        for member in range(2):
            for half in range(2):
                wide = x_ext[member, at, half]
                for i in range(0, PARTS, 2):
                    rows = turn(wide, -FINE * (i + 1))[:, :BLOCK]
                    behind[side, half, member, i // 2] = rows
        for place in range(2):
            taps_of(taps_b, side, place, f_wide, place, step, 1 - FINE)

    def pulled_and_cross(windows, rows, side, half):
        lhs = ahead[windows, rows].reshape(4 * size, BLOCK)
        tops = jnp.concatenate([lhs[:size], lhs[2 * size : 3 * size]], axis=0)
        low = nt_dot(tops, tile(taps_a, side, 1, half))
        if half is None:
            high = nt_dot(lhs, tile(taps_a, side, 0, half))
        pulled, cross = [], None
        for member in range(2):
            at = 2 * size * member
            part = lhs[at : at + 2 * size]
            other = tile(taps_a, side, 2 + member, half)
            if half is None:
                first, both = high[at : at + 2 * size], nt_dot(part, other)
            else:
                wide = jnp.concatenate([tile(taps_a, side, 0, half), other], axis=0)
                wide = nt_dot(part, wide)
                first, both = wide[:, :128], wide[:, 128:]
            low_part = low[size * member : size * member + size]
            pulled.append(first[:size] + first[size:] + low_part)
            both = both[:size] + both[size:]
            cross = both if cross is None else cross + both
        return pulled[0], pulled[1], cross

    def convolved(windows, rows, side, half):
        lhs = behind[windows, rows].reshape(2 * size, BLOCK)
        high, low = tile(taps_b, side, 0, half), tile(taps_b, side, 1, half)
        if half is None:
            both = nt_dot(lhs, high) + nt_dot(lhs, low)
        else:
            both = nt_dot(lhs, jnp.concatenate([high, low], axis=0))
            both = both[:, :128] + both[:, 128:]
        return both[:size], both[size:]

    def products(first, multiply, near_rows, side, start):
        jobs = [(0, near_rows, side, None), (0, 1 - near_rows, side, 0)]
        if not start:
            jobs = [(1, 1 - near_rows, 1 - side, None), (1, near_rows, 1 - side, 1)] + jobs
        for far, rows, taps_side, half in jobs:
            lanes = slice(None) if half is None else slice(128 * half, 128 * half + 128)
            for k, value in enumerate(multiply(side, rows, taps_side, half)):
                if start:
                    acc[far, first + k, rows, :, lanes] = value
                else:
                    acc[far, first + k, rows, :, lanes] += value
        if start:
            acc[1, first : first + (2 if first == 0 else 3)] = jnp.zeros(
                (2 if first == 0 else 3, 2, size, BLOCK), F32
            )

    def run(first, multiply, near_rows, build, steps):
        def pair(i, carry):
            products(first, multiply, near_rows, 1, False)
            build(0, 2 * i + 2)
            products(first, multiply, near_rows, 0, False)
            build(1, 2 * i + 3)
            return carry

        build(0, 0)
        products(first, multiply, near_rows, 0, True)
        build(1, 1)
        lax.fori_loop(0, steps // 2, pair, 0)
        pl.when(steps % 2 == 1)(lambda: products(first, multiply, near_rows, 1, False))

    run(0, convolved, 0, behind_build, plane)
    run(2, pulled_and_cross, 1, ahead_build, PLANES - 1 - plane)

    lanes = lax.broadcasted_iota(jnp.int32, (RING, BLOCK), 1)
    lanes = lanes // 128 * 8 + lanes % 8
    lines = lax.broadcasted_iota(jnp.int32, (RING, BLOCK), 0)
    source = lax.broadcasted_iota(jnp.int32, (BLOCK, BLOCK), 0) % 128
    source = source // 16 * 2 + source // 8 % 2
    target = lax.broadcasted_iota(jnp.int32, (BLOCK, BLOCK), 1)
    total = jnp.zeros((5 * RING, BLOCK), F32)
    for i in range(PARTS):
        pieces = []
        for k in range(5):
            near, far = (
                jnp.concatenate([acc[side, k, half, 8 * i : 8 * i + 8] for half in range(2)], axis=0)
                for side in range(2)
            )
            value = jnp.where(lines + lanes < RING if k < 2 else lines >= lanes, near, far)
            for bit in (1, 2, 4, 8):
                moved = pltpu.roll(value, bit if k < 2 else RING - bit, 0)
                value = jnp.where((lanes & bit) != 0, moved, value)
            pieces.append(value)
        pick = (source + FINE * i == target).astype(BF16)
        both = jnp.concatenate(split(jnp.concatenate(pieces, axis=0)), axis=0)
        both = jnp.dot(both, pick, preferred_element_type=F32)
        total = total + (both[: 5 * RING] + both[5 * RING :])
    for k in range(5):
        for half in range(2):
            part = total[RING * k : RING * k + RING, 128 * half : 128 * half + 128]
            out_ref[pl.ds(2 * k + half, RING, stride=10), :] = part


def middle(arrived, plane):
    return pl.pallas_call(
        middle_kernel,
        out_shape=jax.ShapeDtypeStruct((10 * RING, 128), F32),
        in_specs=[
            pl.BlockSpec(memory_space=pltpu.SMEM),
            pl.BlockSpec(memory_space=pltpu.VMEM),
        ],
        out_specs=pl.BlockSpec(memory_space=pltpu.VMEM),
        scratch_shapes=[
            pltpu.VMEM((2, PLANES, 2, 16, 384), BF16),
            pltpu.VMEM((2, PLANES, 2, 16, 384), BF16),
            pltpu.VMEM((2, PLANES, 2, 16, 384), BF16),
            pltpu.VMEM((2, 2, PLANES, 2, 16, 2 * BLOCK), BF16),
            pltpu.VMEM((2, PLANES, 2, 16, 2 * BLOCK), BF16),
            pltpu.VMEM((2, 4, 2, FINE // 2, 16, BLOCK), BF16),
            pltpu.VMEM((2, 2, 2, FINE // 2, 16, BLOCK), BF16),
            pltpu.VMEM((2, 2, 2, 2, PARTS // 2, 16, BLOCK), BF16),
            pltpu.VMEM((2, 2, 2, PARTS // 2, 16, BLOCK), BF16),
            pltpu.VMEM((2, 5, 2, PARTS * 8, BLOCK), F32),
        ],
        compiler_params=pltpu.CompilerParams(vmem_limit_bytes=32 * 1024 * 1024),
    )(plane, arrived)


VMEM = pl.BlockSpec(memory_space=pltpu.VMEM)
SMALL = pltpu.CompilerParams(vmem_limit_bytes=4 * 1024 * 1024)


def source_kernel(signal_ref, filter_ref, skip_ref, out_ref, aside_ref):
    filters = jnp.concatenate([filter_ref[i] for i in range(4)] * 2, axis=0)
    line = 0
    for value in [signal_ref[RING * i : RING * i + RING] for i in range(4)] + [filters]:
        for half in range(2):
            part = value[:, 128 * half : 128 * half + 128]
            out_ref[pl.ds(line, RING, stride=10), :] = part
            line += 1
    across = lax.broadcasted_iota(jnp.int32, (32, 32), 1)
    down = lax.broadcasted_iota(jnp.int32, (32, 32), 0)
    skip = jnp.where(across == down, skip_ref[...], 0.0).sum(axis=1, keepdims=True)
    aside_ref[...] = jnp.broadcast_to(skip, aside_ref.shape)


def source(signals, filters, skip):
    return pl.pallas_call(
        source_kernel,
        out_shape=(
            jax.ShapeDtypeStruct((10 * RING, 128), F32),
            jax.ShapeDtypeStruct((32, BLOCK), F32),
        ),
        in_specs=[VMEM] * 3,
        out_specs=[VMEM] * 2,
        compiler_params=SMALL,
    )(signals, filters, skip)


def spread_kernel(in_ref, out_ref):
    for line in range(10):
        rows = in_ref[pl.ds(line, RING, stride=10), :]
        for plane in range(PLANES):
            out_ref[plane, line] = rows


def spread(ring):
    return pl.pallas_call(
        spread_kernel,
        out_shape=jax.ShapeDtypeStruct((PLANES, 10, RING, 128), F32),
        in_specs=[VMEM],
        out_specs=VMEM,
        compiler_params=SMALL,
    )(ring)


def sums_kernel(b_ref, out_ref):
    for half in range(2):
        rows = b_ref[pl.ds(8 + half, RING, stride=10), :]
        out_ref[:, 128 * half : 128 * half + 128] = rows[:8] + rows[8:]


def sums(returned):
    return pl.pallas_call(
        sums_kernel,
        out_shape=jax.ShapeDtypeStruct((8, BLOCK), F32),
        in_specs=[VMEM],
        out_specs=VMEM,
        compiler_params=SMALL,
    )(returned)


def final_kernel(slot_ref, b_ref, signal_ref, up_ref, skip_ref, shares_ref, gi_ref, gg_ref, gf_ref):
    def channels(first):
        halves = [
            jnp.concatenate(
                [b_ref[pl.ds(first + 2 * member + half, RING, stride=10), :] for member in range(2)],
                axis=0,
            )
            for half in range(2)
        ]
        return jnp.concatenate(halves, axis=1)

    x, mixed = signal_ref[:32], signal_ref[32:]
    up, skip = up_ref[...].astype(F32), skip_ref[...]
    gg_ref[...] = (up * (channels(0) + skip * x)).astype(BF16)
    gi_ref[...] = (channels(4) + skip * mixed).astype(BF16)
    taps = (shares_ref[0] + shares_ref[1]) + (shares_ref[2] + shares_ref[3])
    slot = slot_ref[0]
    own = taps[:2]
    for other in range(1, 4):
        own = jnp.where(slot == other, taps[2 * other : 2 * other + 2], own)
    gf_ref[...] = own * (1.0 / math.sqrt(BLOCKS * BLOCK))


def final(slot, returned, signals, upstream, skip, shares):
    piece = jax.ShapeDtypeStruct((32, BLOCK), BF16)
    return pl.pallas_call(
        final_kernel,
        out_shape=(piece, piece, jax.ShapeDtypeStruct((2, BLOCK), F32)),
        in_specs=[pl.BlockSpec(memory_space=pltpu.SMEM)] + [VMEM] * 5,
        out_specs=[VMEM] * 3,
        compiler_params=SMALL,
    )(slot, returned, signals, upstream, skip, shares)


def exchange(rows, groups=None):
    members = BLOCKS if groups is None else len(groups[0])
    flat = lax.all_to_all(
        rows.reshape(members, 1, -1),
        "seq",
        split_axis=0,
        concat_axis=0,
        tiled=True,
        axis_index_groups=groups,
    )
    return flat.reshape(rows.shape)


def body(inputs, gate_values, filters, skip_weight, grad_out):
    rings = [[RING * plane + z for z in range(RING)] for plane in range(PLANES)]
    planes = [[RING * plane + z for plane in range(PLANES)] for z in range(RING)]
    mixed = grad_out.astype(F32) * gate_values.astype(F32)
    signals = jnp.concatenate([inputs.astype(F32), mixed], axis=0)
    every_filter = lax.all_gather(filters, "chan", axis=0)
    leaving, skip = source(signals, every_filter, skip_weight[None, :])
    plane = (lax.axis_index("seq") >> 4).astype(jnp.int32).reshape(1)
    slot = lax.axis_index("chan").astype(jnp.int32).reshape(1)
    leaving, plane, slot = lax.optimization_barrier((leaving, plane, slot))
    arrived = exchange(spread(exchange(leaving, rings)), planes)
    returned = exchange(middle(arrived, plane), rings)
    shares = lax.all_gather(sums(returned), "chan", axis=0)
    return final(slot, returned, signals, grad_out, skip, shares)


def solution(mesh):
    placed = (P("chan", "seq"), P("chan", "seq"), P("chan", "seq"), P("chan"), P("chan", "seq"))
    return jax.shard_map(
        body,
        mesh=mesh,
        in_specs=placed,
        out_specs=(P("chan", "seq"), P("chan", "seq"), P("chan", "seq")),
        check_vma=False,
    )
```

```python
import functools
import math

import jax
import jax.numpy as jnp
from jax import lax
from jax.experimental import pallas as pl
from jax.experimental.pallas import tpu as pltpu
from jax.sharding import PartitionSpec as P

BLOCK = 256
BLOCKS = 128
FINE = 16
PARTS = BLOCK // FINE
RING = 16
PLANES = 8
F32 = jnp.float32
BF16 = jnp.bfloat16


def split(value):
    high = value.astype(BF16)
    return high, (value - high.astype(F32)).astype(BF16)


def rows_down(value):
    row = lax.broadcasted_iota(jnp.int32, value.shape, 0)
    return jnp.where(row == 0, 0.0, pltpu.roll(value, 1, 0))


def rows_up(value):
    row = lax.broadcasted_iota(jnp.int32, value.shape, 0)
    return jnp.where(row == BLOCKS - 1, 0.0, pltpu.roll(value, BLOCKS - 1, 0))


def nt_dot(left, right):
    return lax.dot_general(
        left, right, (((1,), (1,)), ((), ())), preferred_element_type=F32
    )


def middle_kernel(plane_ref, a_ref, out_ref, h_wide, x_wide, f_wide, g_ext, x_ext, taps_a, taps_b, ahead, behind, acc):
    plane = plane_ref[0]

    def signal(first):
        halves = [a_ref[:, first + half].reshape(BLOCKS, 128) for half in range(2)]
        return jnp.concatenate(halves, axis=1)

    def turn(value, shift):
        size = value.shape[1]
        return pltpu.roll(value, shift % size, 1) if shift % size else value

    def pairs(value, shift):
        parts = [part.reshape(PLANES, 2, 8, -1) for part in (value, turn(value, shift))]
        return jnp.concatenate(parts, axis=2)

    h = signal(8)
    h_down = rows_down(h)
    across = lax.broadcasted_iota(jnp.int32, (BLOCK, BLOCK), 1)
    down = lax.broadcasted_iota(jnp.int32, (BLOCK, BLOCK), 0)
    mirror = (across + down == BLOCK - 1).astype(BF16)
    for place, piece in enumerate(split(h)):
        flipped = jnp.dot(piece, mirror, preferred_element_type=F32)
        wide = jnp.concatenate([rows_down(flipped)[:, :128], flipped], axis=1)
        f_wide[place] = pairs(wide, 1).astype(BF16)
    for place, piece in enumerate(split(pairs(jnp.concatenate([h_down[:, 128:], h], axis=1), 1))):
        h_wide[place] = piece
    for member in range(2):
        x = signal(2 * member)
        g = signal(4 + 2 * member)
        x_down = rows_down(x)
        x_wide[member] = pairs(jnp.concatenate([x_down[:, 128:], x], axis=1), 1).astype(BF16)
        x_ext[member] = pairs(jnp.concatenate([x_down, x], axis=1), -FINE).astype(BF16)
        wide = pairs(jnp.concatenate([g, rows_up(g)], axis=1), -FINE)
        for place, piece in enumerate(split(wide)):
            g_ext[member, place] = piece

    size = PARTS * 8

    def taps_of(ref, side, slot, wide_ref, place, step, least):
        for half in range(2):
            wide = wide_ref[place, step, half]
            for n in range(0, FINE, 2):
                ref[side, slot, half, n // 2] = turn(wide, least + n)[:, 128:]

    def tile(ref, side, slot, half):
        if half is None:
            return ref[side, slot].reshape(BLOCK, BLOCK)
        return ref[side, slot, half].reshape(128, BLOCK)

    def ahead_build(side, step):
        step = jnp.minimum(step, PLANES - 1)
        at = jnp.minimum(plane + step, PLANES - 1)
        for member in range(2):
            for place in range(2):
                for half in range(2):
                    wide = g_ext[member, place, at, half]
                    for i in range(0, PARTS, 2):
                        rows = turn(wide, -FINE * i)[:, :BLOCK]
                        ahead[side, half, member, place, i // 2] = rows
        for place in range(2):
            taps_of(taps_a, side, place, h_wide, place, step, 0)
            taps_of(taps_a, side, 2 + place, x_wide, place, step, 0)

    def behind_build(side, step):
        step = jnp.minimum(step, PLANES - 1)
        at = jnp.maximum(plane - step, 0)
        for member in range(2):
            for half in range(2):
                wide = x_ext[member, at, half]
                for i in range(0, PARTS, 2):
                    rows = turn(wide, -FINE * (i + 1))[:, :BLOCK]
                    behind[side, half, member, i // 2] = rows
        for place in range(2):
            taps_of(taps_b, side, place, f_wide, place, step, 1 - FINE)

    def pulled_and_cross(windows, rows, side, half):
        lhs = ahead[windows, rows].reshape(4 * size, BLOCK)
        tops = jnp.concatenate([lhs[:size], lhs[2 * size : 3 * size]], axis=0)
        low = nt_dot(tops, tile(taps_a, side, 1, half))
        if half is None:
            high = nt_dot(lhs, tile(taps_a, side, 0, half))
        pulled, cross = [], None
        for member in range(2):
            at = 2 * size * member
            part = lhs[at : at + 2 * size]
            other = tile(taps_a, side, 2 + member, half)
            if half is None:
                first, both = high[at : at + 2 * size], nt_dot(part, other)
            else:
                wide = jnp.concatenate([tile(taps_a, side, 0, half), other], axis=0)
                wide = nt_dot(part, wide)
                first, both = wide[:, :128], wide[:, 128:]
            low_part = low[size * member : size * member + size]
            pulled.append(first[:size] + first[size:] + low_part)
            both = both[:size] + both[size:]
            cross = both if cross is None else cross + both
        return pulled[0], pulled[1], cross

    def convolved(windows, rows, side, half):
        lhs = behind[windows, rows].reshape(2 * size, BLOCK)
        high, low = tile(taps_b, side, 0, half), tile(taps_b, side, 1, half)
        if half is None:
            both = nt_dot(lhs, high) + nt_dot(lhs, low)
        else:
            both = nt_dot(lhs, jnp.concatenate([high, low], axis=0))
            both = both[:, :128] + both[:, 128:]
        return both[:size], both[size:]

    def products(first, multiply, near_rows, side, start):
        jobs = [(0, near_rows, side, None), (0, 1 - near_rows, side, 0)]
        if not start:
            jobs = [(1, 1 - near_rows, 1 - side, None), (1, near_rows, 1 - side, 1)] + jobs
        for far, rows, taps_side, half in jobs:
            lanes = slice(None) if half is None else slice(128 * half, 128 * half + 128)
            for k, value in enumerate(multiply(side, rows, taps_side, half)):
                if start:
                    acc[far, first + k, rows, :, lanes] = value
                else:
                    acc[far, first + k, rows, :, lanes] += value
        if start:
            acc[1, first : first + (2 if first == 0 else 3)] = jnp.zeros(
                (2 if first == 0 else 3, 2, size, BLOCK), F32
            )

    def run(first, multiply, near_rows, build, steps):
        def pair(i, carry):
            products(first, multiply, near_rows, 1, False)
            build(0, 2 * i + 2)
            products(first, multiply, near_rows, 0, False)
            build(1, 2 * i + 3)
            return carry

        build(0, 0)
        products(first, multiply, near_rows, 0, True)
        build(1, 1)
        lax.fori_loop(0, steps // 2, pair, 0)
        pl.when(steps % 2 == 1)(lambda: products(first, multiply, near_rows, 1, False))

    run(0, convolved, 0, behind_build, plane)
    run(2, pulled_and_cross, 1, ahead_build, PLANES - 1 - plane)

    lanes = lax.broadcasted_iota(jnp.int32, (RING, BLOCK), 1)
    lanes = lanes // 128 * 8 + lanes % 8
    lines = lax.broadcasted_iota(jnp.int32, (RING, BLOCK), 0)
    source = lax.broadcasted_iota(jnp.int32, (BLOCK, BLOCK), 0) % 128
    source = source // 16 * 2 + source // 8 % 2
    target = lax.broadcasted_iota(jnp.int32, (BLOCK, BLOCK), 1)
    total = jnp.zeros((5 * RING, BLOCK), F32)
    for i in range(PARTS):
        pieces = []
        for k in range(5):
            near, far = (
                jnp.concatenate([acc[side, k, half, 8 * i : 8 * i + 8] for half in range(2)], axis=0)
                for side in range(2)
            )
            value = jnp.where(lines + lanes < RING if k < 2 else lines >= lanes, near, far)
            for bit in (1, 2, 4, 8):
                moved = pltpu.roll(value, bit if k < 2 else RING - bit, 0)
                value = jnp.where((lanes & bit) != 0, moved, value)
            pieces.append(value)
        pick = (source + FINE * i == target).astype(BF16)
        both = jnp.concatenate(split(jnp.concatenate(pieces, axis=0)), axis=0)
        both = jnp.dot(both, pick, preferred_element_type=F32)
        total = total + (both[: 5 * RING] + both[5 * RING :])
    for k in range(5):
        for half in range(2):
            part = total[RING * k : RING * k + RING, 128 * half : 128 * half + 128]
            out_ref[pl.ds(2 * k + half, RING, stride=10), :] = part


def middle(arrived, plane):
    return pl.pallas_call(
        middle_kernel,
        out_shape=jax.ShapeDtypeStruct((10 * RING, 128), F32),
        in_specs=[
            pl.BlockSpec(memory_space=pltpu.SMEM),
            pl.BlockSpec(memory_space=pltpu.VMEM),
        ],
        out_specs=pl.BlockSpec(memory_space=pltpu.VMEM),
        scratch_shapes=[
            pltpu.VMEM((2, PLANES, 2, 16, 384), BF16),
            pltpu.VMEM((2, PLANES, 2, 16, 384), BF16),
            pltpu.VMEM((2, PLANES, 2, 16, 384), BF16),
            pltpu.VMEM((2, 2, PLANES, 2, 16, 2 * BLOCK), BF16),
            pltpu.VMEM((2, PLANES, 2, 16, 2 * BLOCK), BF16),
            pltpu.VMEM((2, 4, 2, FINE // 2, 16, BLOCK), BF16),
            pltpu.VMEM((2, 2, 2, FINE // 2, 16, BLOCK), BF16),
            pltpu.VMEM((2, 2, 2, 2, PARTS // 2, 16, BLOCK), BF16),
            pltpu.VMEM((2, 2, 2, PARTS // 2, 16, BLOCK), BF16),
            pltpu.VMEM((2, 5, 2, PARTS * 8, BLOCK), F32),
        ],
        compiler_params=pltpu.CompilerParams(vmem_limit_bytes=32 * 1024 * 1024),
        cost_estimate=pl.CostEstimate(
            flops=2 * 116 * BLOCK**3, bytes_accessed=720 * 1024, transcendentals=0
        ),
    )(plane, arrived)


VMEM = pl.BlockSpec(memory_space=pltpu.VMEM)
SMALL = pltpu.CompilerParams(vmem_limit_bytes=4 * 1024 * 1024)


def source_kernel(signal_ref, filter_ref, out_ref):
    filters = jnp.concatenate([filter_ref[i] for i in range(4)] * 2, axis=0)
    line = 0
    for value in [signal_ref[RING * i : RING * i + RING] for i in range(4)] + [filters]:
        for half in range(2):
            part = value[:, 128 * half : 128 * half + 128]
            out_ref[pl.ds(line, RING, stride=10), :] = part
            line += 1


def source(signals, filters):
    return pl.pallas_call(
        source_kernel,
        out_shape=jax.ShapeDtypeStruct((10 * RING, 128), F32),
        in_specs=[VMEM] * 2,
        out_specs=VMEM,
        compiler_params=SMALL,
    )(signals, filters)


def column_kernel(skip_ref, out_ref):
    across = lax.broadcasted_iota(jnp.int32, (32, 32), 1)
    down = lax.broadcasted_iota(jnp.int32, (32, 32), 0)
    skip = jnp.where(across == down, skip_ref[...], 0.0).sum(axis=1, keepdims=True)
    out_ref[...] = jnp.broadcast_to(skip, out_ref.shape)


def column(skip):
    return pl.pallas_call(
        column_kernel,
        out_shape=jax.ShapeDtypeStruct((32, BLOCK), F32),
        in_specs=[VMEM],
        out_specs=VMEM,
        compiler_params=SMALL,
    )(skip[None, :])


def spread_kernel(in_ref, out_ref):
    for line in range(10):
        rows = in_ref[pl.ds(line, RING, stride=10), :]
        for plane in range(PLANES):
            out_ref[plane, line] = rows


def spread(ring):
    return pl.pallas_call(
        spread_kernel,
        out_shape=jax.ShapeDtypeStruct((PLANES, 10, RING, 128), F32),
        in_specs=[VMEM],
        out_specs=VMEM,
        compiler_params=SMALL,
    )(ring)


def sums_kernel(b_ref, out_ref):
    for half in range(2):
        rows = b_ref[pl.ds(8 + half, RING, stride=10), :]
        out_ref[:, 128 * half : 128 * half + 128] = rows[:8] + rows[8:]


def sums(returned):
    return pl.pallas_call(
        sums_kernel,
        out_shape=jax.ShapeDtypeStruct((8, BLOCK), F32),
        in_specs=[VMEM],
        out_specs=VMEM,
        compiler_params=SMALL,
    )(returned)


def final_kernel(slot_ref, b_ref, signal_ref, up_ref, skip_ref, shares_ref, gi_ref, gg_ref, gf_ref):
    def channels(first):
        halves = [
            jnp.concatenate(
                [b_ref[pl.ds(first + 2 * member + half, RING, stride=10), :] for member in range(2)],
                axis=0,
            )
            for half in range(2)
        ]
        return jnp.concatenate(halves, axis=1)

    x, mixed = signal_ref[:32], signal_ref[32:]
    up, skip = up_ref[...].astype(F32), skip_ref[...]
    gg_ref[...] = (up * (channels(0) + skip * x)).astype(BF16)
    gi_ref[...] = (channels(4) + skip * mixed).astype(BF16)
    taps = (shares_ref[0] + shares_ref[1]) + (shares_ref[2] + shares_ref[3])
    slot = slot_ref[0]
    own = taps[:2]
    for other in range(1, 4):
        own = jnp.where(slot == other, taps[2 * other : 2 * other + 2], own)
    gf_ref[...] = own * (1.0 / math.sqrt(BLOCKS * BLOCK))


def final(slot, returned, signals, upstream, skip, shares):
    piece = jax.ShapeDtypeStruct((32, BLOCK), BF16)
    return pl.pallas_call(
        final_kernel,
        out_shape=(piece, piece, jax.ShapeDtypeStruct((2, BLOCK), F32)),
        in_specs=[pl.BlockSpec(memory_space=pltpu.SMEM)] + [VMEM] * 5,
        out_specs=[VMEM] * 3,
        compiler_params=SMALL,
    )(slot, returned, signals, upstream, skip, shares)


def exchange(rows, groups=None):
    members = BLOCKS if groups is None else len(groups[0])
    flat = lax.all_to_all(
        rows.reshape(members, 1, -1),
        "seq",
        split_axis=0,
        concat_axis=0,
        tiled=True,
        axis_index_groups=groups,
    )
    return flat.reshape(rows.shape)


def body(inputs, gate_values, filters, skip_weight, grad_out):
    rings = [[RING * plane + z for z in range(RING)] for plane in range(PLANES)]
    planes = [[RING * plane + z for plane in range(PLANES)] for z in range(RING)]
    mixed = grad_out.astype(F32) * gate_values.astype(F32)
    signals = jnp.concatenate([inputs.astype(F32), mixed], axis=0)
    every_filter = lax.all_gather(filters, "chan", axis=0)
    leaving = source(signals, every_filter)
    plane = (lax.axis_index("seq") >> 4).astype(jnp.int32).reshape(1)
    slot = lax.axis_index("chan").astype(jnp.int32).reshape(1)
    leaving, plane, slot = lax.optimization_barrier((leaving, plane, slot))
    arrived = exchange(spread(exchange(leaving, rings)), planes)
    results, skip = lax.optimization_barrier((middle(arrived, plane), column(skip_weight)))
    returned = exchange(results, rings)
    shares = lax.all_gather(sums(returned), "chan", axis=0)
    return final(slot, returned, signals, grad_out, skip, shares)


def solution(mesh):
    placed = (P("chan", "seq"), P("chan", "seq"), P("chan", "seq"), P("chan"), P("chan", "seq"))
    return jax.shard_map(
        body,
        mesh=mesh,
        in_specs=placed,
        out_specs=(P("chan", "seq"), P("chan", "seq"), P("chan", "seq")),
        check_vma=False,
    )
```

```python
import functools
import math

import jax
import jax.numpy as jnp
from jax import lax
from jax.experimental import pallas as pl
from jax.experimental.pallas import tpu as pltpu
from jax.sharding import PartitionSpec as P

BLOCK = 256
BLOCKS = 128
FINE = 16
PARTS = BLOCK // FINE
RING = 16
PLANES = 8
F32 = jnp.float32
BF16 = jnp.bfloat16


def split(value):
    high = value.astype(BF16)
    return high, (value - high.astype(F32)).astype(BF16)


def rows_down(value):
    row = lax.broadcasted_iota(jnp.int32, value.shape, 0)
    return jnp.where(row == 0, 0.0, pltpu.roll(value, 1, 0))


def rows_up(value):
    row = lax.broadcasted_iota(jnp.int32, value.shape, 0)
    return jnp.where(row == BLOCKS - 1, 0.0, pltpu.roll(value, BLOCKS - 1, 0))


def nt_dot(left, right):
    return lax.dot_general(
        left, right, (((1,), (1,)), ((), ())), preferred_element_type=F32
    )


def middle_kernel(plane_ref, a_ref, out_ref, h_wide, x_wide, f_wide, g_ext, x_ext, taps_a, taps_b, ahead, behind, acc):
    plane = plane_ref[0]

    def signal(first):
        halves = [a_ref[:, first + half].reshape(BLOCKS, 128) for half in range(2)]
        return jnp.concatenate(halves, axis=1)

    def turn(value, shift):
        size = value.shape[1]
        return pltpu.roll(value, shift % size, 1) if shift % size else value

    def pairs(value, shift):
        parts = [part.reshape(PLANES, 2, 8, -1) for part in (value, turn(value, shift))]
        return jnp.concatenate(parts, axis=2)

    h = signal(8)
    h_down = rows_down(h)
    across = lax.broadcasted_iota(jnp.int32, (BLOCK, BLOCK), 1)
    down = lax.broadcasted_iota(jnp.int32, (BLOCK, BLOCK), 0)
    mirror = (across + down == BLOCK - 1).astype(BF16)
    for place, piece in enumerate(split(h)):
        flipped = jnp.dot(piece, mirror, preferred_element_type=F32)
        wide = jnp.concatenate([rows_down(flipped)[:, :128], flipped], axis=1)
        f_wide[place] = pairs(wide, 1).astype(BF16)
    for place, piece in enumerate(split(pairs(jnp.concatenate([h_down[:, 128:], h], axis=1), 1))):
        h_wide[place] = piece
    for member in range(2):
        x = signal(2 * member)
        g = signal(4 + 2 * member)
        x_down = rows_down(x)
        x_wide[member] = pairs(jnp.concatenate([x_down[:, 128:], x], axis=1), 1).astype(BF16)
        x_ext[member] = pairs(jnp.concatenate([x_down, x], axis=1), -FINE).astype(BF16)
        wide = pairs(jnp.concatenate([g, rows_up(g)], axis=1), -FINE)
        for place, piece in enumerate(split(wide)):
            g_ext[member, place] = piece

    size = PARTS * 8

    def taps_of(ref, side, slot, wide_ref, place, step, least):
        for half in range(2):
            wide = wide_ref[place, step, half]
            for n in range(0, FINE, 2):
                ref[side, slot, half, n // 2] = turn(wide, least + n)[:, 128:]

    def tile(ref, side, slot, half):
        if half is None:
            return ref[side, slot].reshape(BLOCK, BLOCK)
        return ref[side, slot, half].reshape(128, BLOCK)

    def ahead_build(side, step):
        step = jnp.minimum(step, PLANES - 1)
        at = jnp.minimum(plane + step, PLANES - 1)
        for member in range(2):
            for place in range(2):
                for half in range(2):
                    wide = g_ext[member, place, at, half]
                    for i in range(0, PARTS, 2):
                        rows = turn(wide, -FINE * i)[:, :BLOCK]
                        ahead[side, half, member, place, i // 2] = rows
        for place in range(2):
            taps_of(taps_a, side, place, h_wide, place, step, 0)
            taps_of(taps_a, side, 2 + place, x_wide, place, step, 0)

    def behind_build(side, step):
        step = jnp.minimum(step, PLANES - 1)
        at = jnp.maximum(plane - step, 0)
        for member in range(2):
            for half in range(2):
                wide = x_ext[member, at, half]
                for i in range(0, PARTS, 2):
                    rows = turn(wide, -FINE * (i + 1))[:, :BLOCK]
                    behind[side, half, member, i // 2] = rows
        for place in range(2):
            taps_of(taps_b, side, place, f_wide, place, step, 1 - FINE)

    def pulled_and_cross(windows, rows, side, half):
        lhs = ahead[windows, rows].reshape(4 * size, BLOCK)
        tops = jnp.concatenate([lhs[:size], lhs[2 * size : 3 * size]], axis=0)
        low = nt_dot(tops, tile(taps_a, side, 1, half))
        if half is None:
            high = nt_dot(lhs, tile(taps_a, side, 0, half))
        pulled, cross = [], None
        for member in range(2):
            at = 2 * size * member
            part = lhs[at : at + 2 * size]
            other = tile(taps_a, side, 2 + member, half)
            if half is None:
                first, both = high[at : at + 2 * size], nt_dot(part, other)
            else:
                wide = jnp.concatenate([tile(taps_a, side, 0, half), other], axis=0)
                wide = nt_dot(part, wide)
                first, both = wide[:, :128], wide[:, 128:]
            low_part = low[size * member : size * member + size]
            pulled.append(first[:size] + first[size:] + low_part)
            both = both[:size] + both[size:]
            cross = both if cross is None else cross + both
        return pulled[0], pulled[1], cross

    def convolved(windows, rows, side, half):
        lhs = behind[windows, rows].reshape(2 * size, BLOCK)
        high, low = tile(taps_b, side, 0, half), tile(taps_b, side, 1, half)
        if half is None:
            both = nt_dot(lhs, high) + nt_dot(lhs, low)
        else:
            both = nt_dot(lhs, jnp.concatenate([high, low], axis=0))
            both = both[:, :128] + both[:, 128:]
        return both[:size], both[size:]

    def products(first, multiply, near_rows, side, start):
        jobs = [(0, near_rows, side, None), (0, 1 - near_rows, side, 0)]
        if not start:
            jobs = [(1, 1 - near_rows, 1 - side, None), (1, near_rows, 1 - side, 1)] + jobs
        for far, rows, taps_side, half in jobs:
            lanes = slice(None) if half is None else slice(128 * half, 128 * half + 128)
            for k, value in enumerate(multiply(side, rows, taps_side, half)):
                if start:
                    acc[far, first + k, rows, :, lanes] = value
                else:
                    acc[far, first + k, rows, :, lanes] += value
        if start:
            acc[1, first : first + (2 if first == 0 else 3)] = jnp.zeros(
                (2 if first == 0 else 3, 2, size, BLOCK), F32
            )

    def run(first, multiply, near_rows, build, steps):
        def pair(i, carry):
            products(first, multiply, near_rows, 1, False)
            build(0, 2 * i + 2)
            products(first, multiply, near_rows, 0, False)
            build(1, 2 * i + 3)
            return carry

        build(0, 0)
        products(first, multiply, near_rows, 0, True)
        build(1, 1)
        lax.fori_loop(0, steps // 2, pair, 0)
        pl.when(steps % 2 == 1)(lambda: products(first, multiply, near_rows, 1, False))

    run(0, convolved, 0, behind_build, plane)
    run(2, pulled_and_cross, 1, ahead_build, PLANES - 1 - plane)

    lanes = lax.broadcasted_iota(jnp.int32, (RING, BLOCK), 1)
    lanes = lanes // 128 * 8 + lanes % 8
    lines = lax.broadcasted_iota(jnp.int32, (RING, BLOCK), 0)
    source = lax.broadcasted_iota(jnp.int32, (BLOCK, BLOCK), 0) % 128
    source = source // 16 * 2 + source // 8 % 2
    target = lax.broadcasted_iota(jnp.int32, (BLOCK, BLOCK), 1)
    total = jnp.zeros((5 * RING, BLOCK), F32)
    for i in range(PARTS):
        pieces = []
        for k in range(5):
            near, far = (
                jnp.concatenate([acc[side, k, half, 8 * i : 8 * i + 8] for half in range(2)], axis=0)
                for side in range(2)
            )
            value = jnp.where(lines + lanes < RING if k < 2 else lines >= lanes, near, far)
            for bit in (1, 2, 4, 8):
                moved = pltpu.roll(value, bit if k < 2 else RING - bit, 0)
                value = jnp.where((lanes & bit) != 0, moved, value)
            pieces.append(value)
        pick = (source + FINE * i == target).astype(BF16)
        both = jnp.concatenate(split(jnp.concatenate(pieces, axis=0)), axis=0)
        both = jnp.dot(both, pick, preferred_element_type=F32)
        total = total + (both[: 5 * RING] + both[5 * RING :])
    for k in range(5):
        for half in range(2):
            part = total[RING * k : RING * k + RING, 128 * half : 128 * half + 128]
            out_ref[pl.ds(2 * k + half, RING, stride=10), :] = part


def middle(arrived, plane):
    return pl.pallas_call(
        middle_kernel,
        out_shape=jax.ShapeDtypeStruct((10 * RING, 128), F32),
        in_specs=[
            pl.BlockSpec(memory_space=pltpu.SMEM),
            pl.BlockSpec(memory_space=pltpu.VMEM),
        ],
        out_specs=pl.BlockSpec(memory_space=pltpu.VMEM),
        scratch_shapes=[
            pltpu.VMEM((2, PLANES, 2, 16, 384), BF16),
            pltpu.VMEM((2, PLANES, 2, 16, 384), BF16),
            pltpu.VMEM((2, PLANES, 2, 16, 384), BF16),
            pltpu.VMEM((2, 2, PLANES, 2, 16, 2 * BLOCK), BF16),
            pltpu.VMEM((2, PLANES, 2, 16, 2 * BLOCK), BF16),
            pltpu.VMEM((2, 4, 2, FINE // 2, 16, BLOCK), BF16),
            pltpu.VMEM((2, 2, 2, FINE // 2, 16, BLOCK), BF16),
            pltpu.VMEM((2, 2, 2, 2, PARTS // 2, 16, BLOCK), BF16),
            pltpu.VMEM((2, 2, 2, PARTS // 2, 16, BLOCK), BF16),
            pltpu.VMEM((2, 5, 2, PARTS * 8, BLOCK), F32),
        ],
        compiler_params=pltpu.CompilerParams(vmem_limit_bytes=32 * 1024 * 1024),
        cost_estimate=pl.CostEstimate(
            flops=2 * 116 * BLOCK**3, bytes_accessed=720 * 1024, transcendentals=0
        ),
    )(plane, arrived)


VMEM = pl.BlockSpec(memory_space=pltpu.VMEM)
SMALL = pltpu.CompilerParams(vmem_limit_bytes=4 * 1024 * 1024)


def source_kernel(signal_ref, filter_ref, out_ref):
    filters = jnp.concatenate([filter_ref[i] for i in range(4)] * 2, axis=0)
    line = 0
    for value in [signal_ref[RING * i : RING * i + RING] for i in range(4)] + [filters]:
        for half in range(2):
            part = value[:, 128 * half : 128 * half + 128]
            out_ref[pl.ds(line, RING, stride=10), :] = part
            line += 1


def source(signals, filters):
    return pl.pallas_call(
        source_kernel,
        out_shape=jax.ShapeDtypeStruct((10 * RING, 128), F32),
        in_specs=[VMEM] * 2,
        out_specs=VMEM,
        compiler_params=SMALL,
    )(signals, filters)


def column_kernel(skip_ref, out_ref):
    across = lax.broadcasted_iota(jnp.int32, (32, 32), 1)
    down = lax.broadcasted_iota(jnp.int32, (32, 32), 0)
    skip = jnp.where(across == down, skip_ref[...], 0.0).sum(axis=1, keepdims=True)
    out_ref[...] = jnp.broadcast_to(skip, out_ref.shape)


def column(skip):
    return pl.pallas_call(
        column_kernel,
        out_shape=jax.ShapeDtypeStruct((32, BLOCK), F32),
        in_specs=[VMEM],
        out_specs=VMEM,
        compiler_params=SMALL,
    )(skip[None, :])


def spread_kernel(in_ref, out_ref):
    for line in range(10):
        rows = in_ref[pl.ds(line, RING, stride=10), :]
        for plane in range(PLANES):
            out_ref[plane, line] = rows


def spread(ring):
    return pl.pallas_call(
        spread_kernel,
        out_shape=jax.ShapeDtypeStruct((PLANES, 10, RING, 128), F32),
        in_specs=[VMEM],
        out_specs=VMEM,
        compiler_params=SMALL,
    )(ring)


def sums_kernel(b_ref, out_ref):
    for half in range(2):
        rows = b_ref[pl.ds(8 + half, RING, stride=10), :]
        out_ref[:, 128 * half : 128 * half + 128] = rows[:8] + rows[8:]


def sums(returned):
    return pl.pallas_call(
        sums_kernel,
        out_shape=jax.ShapeDtypeStruct((8, BLOCK), F32),
        in_specs=[VMEM],
        out_specs=VMEM,
        compiler_params=SMALL,
    )(returned)


def final_kernel(slot_ref, b_ref, signal_ref, up_ref, skip_ref, shares_ref, gi_ref, gg_ref, gf_ref):
    def channels(first):
        halves = [
            jnp.concatenate(
                [b_ref[pl.ds(first + 2 * member + half, RING, stride=10), :] for member in range(2)],
                axis=0,
            )
            for half in range(2)
        ]
        return jnp.concatenate(halves, axis=1)

    x, mixed = signal_ref[:32], signal_ref[32:]
    up, skip = up_ref[...].astype(F32), skip_ref[...]
    gg_ref[...] = (up * (channels(0) + skip * x)).astype(BF16)
    gi_ref[...] = (channels(4) + skip * mixed).astype(BF16)
    taps = (shares_ref[0] + shares_ref[1]) + (shares_ref[2] + shares_ref[3])
    slot = slot_ref[0]
    own = taps[:2]
    for other in range(1, 4):
        own = jnp.where(slot == other, taps[2 * other : 2 * other + 2], own)
    gf_ref[...] = own * (1.0 / math.sqrt(BLOCKS * BLOCK))


def final(slot, returned, signals, upstream, skip, shares):
    piece = jax.ShapeDtypeStruct((32, BLOCK), BF16)
    return pl.pallas_call(
        final_kernel,
        out_shape=(piece, piece, jax.ShapeDtypeStruct((2, BLOCK), F32)),
        in_specs=[pl.BlockSpec(memory_space=pltpu.SMEM)] + [VMEM] * 5,
        out_specs=[VMEM] * 3,
        compiler_params=SMALL,
    )(slot, returned, signals, upstream, skip, shares)


def exchange(rows, groups=None):
    members = BLOCKS if groups is None else len(groups[0])
    flat = lax.all_to_all(
        rows.reshape(members, 1, -1),
        "seq",
        split_axis=0,
        concat_axis=0,
        tiled=True,
        axis_index_groups=groups,
    )
    return flat.reshape(rows.shape)


def body(inputs, gate_values, filters, skip_weight, grad_out):
    rings = [[RING * plane + z for z in range(RING)] for plane in range(PLANES)]
    planes = [[RING * plane + z for plane in range(PLANES)] for z in range(RING)]
    mixed = grad_out.astype(F32) * gate_values.astype(F32)
    signals = jnp.concatenate([inputs.astype(F32), mixed], axis=0)
    every_filter = lax.all_gather(filters, "chan", axis=0)
    leaving = source(signals, every_filter)
    plane = (lax.axis_index("seq") >> 4).astype(jnp.int32).reshape(1)
    slot = lax.axis_index("chan").astype(jnp.int32).reshape(1)
    leaving, plane, slot = lax.optimization_barrier((leaving, plane, slot))
    ring, skip = lax.optimization_barrier((exchange(leaving, rings), column(skip_weight)))
    arrived = exchange(spread(ring), planes)
    results = middle(arrived, plane)
    returned = exchange(results, rings)
    shares = lax.all_gather(sums(returned), "chan", axis=0)
    return final(slot, returned, signals, grad_out, skip, shares)


def solution(mesh):
    placed = (P("chan", "seq"), P("chan", "seq"), P("chan", "seq"), P("chan"), P("chan", "seq"))
    return jax.shard_map(
        body,
        mesh=mesh,
        in_specs=placed,
        out_specs=(P("chan", "seq"), P("chan", "seq"), P("chan", "seq")),
        check_vma=False,
    )
```
